128 devices in a mesh: branch: 4 (over x), subtree: 32 (over z, y, core).
Axes of the slice: x: 4, y: 4, z: 4, core: 2. Of those that a mesh axis runs over, the one named last changes fastest.
Arguments:
- vectors: float32 [64, 1048576], P(None, ('branch', 'subtree')), may hold values from -6 to 6
- basis: float32 [32, 1048576], P(None, ('branch', 'subtree')), may hold values from -0.75 to 0.75
- transfer: float32 [16384, 1024], P(('branch', 'subtree')), may hold values from -0.375 to 0.375
- leaf_coupling: float32 [16384, 32, 512], P(('branch', 'subtree')), may hold values from -0.25 to 0.25
- leaf_list: int32 [16384, 16], P(('branch', 'subtree')), may hold values from 0 to 16383, as said below
- leaf_mask: int32 [16384, 16], P(('branch', 'subtree')), may hold values 0 or 1
- parent_coupling: float32 [2048, 32, 1024], P(('branch', 'subtree')), may hold values from -0.1875 to 0.1875
- parent_list: int32 [2048, 32], P(('branch', 'subtree')), may hold values from 0 to 2047, as said below
- parent_mask: int32 [2048, 32], P(('branch', 'subtree')), may hold values 0 or 1
Outputs:
- product: float32 [64, 1048576], P(None, ('branch', 'subtree'))
The draws below stay inside these ranges and needn't reach their ends.
Inputs may be any that keep to these rules, and one draw needn't show every extreme that they name: `leaf_list`: leaf clusters g * 128 to (g + 1) * 128 - 1 belong to device g, g counted over branch then subtree. The 128 rows of one device name leaves of devices of its own branch group only, each of those 32 devices in exactly 64 slots, padded slots included. `parent_list`: parent clusters g * 16 to (g + 1) * 16 - 1 belong to device g, g counted over branch then subtree. The 16 rows of one device name parents of devices with its own subtree index only, those of each of the 4 branch groups in exactly 128 slots, padded slots included.
All inputs are finite; a program needn't handle non-finite values. No bound on the sum of `leaf_mask` or of `parent_mask` on one device may be relied on, other than what follows from the above.
Results may differ from the reference program's by a relative error of at most 0.000065.
Values sent between devices are 32-bit elements; how exact they have to be, the bound alone decides.
No kernel may reach another device: no remote copies, remote signals or barrier semaphores. Data moves between devices by JAX's collectives and lax.ppermute only.
A program may use at most 256 MiB of HBM per device.

```python
import jax
import jax.numpy as jnp
from jax import lax

PTS = 64
K = 32
NV = 64
CHILD = 8
M_LEAF = 16
M_PAR = 32
LEAF_DEV = 128
PAR_DEV = 16
NLEAF = 16384
NPAR = 2048
NPTS = 1048576
CAP = 64
CAPP = 128
N_BRANCH = 4
N_SUBTREE = 32


def spread_lists(key, rows_dev, slots, capacity, by_branch):
    devices = N_BRANCH * N_SUBTREE
    entries = rows_dev * slots
    subkeys = jax.random.split(key, devices + 1)
    grouped = jnp.arange(entries, dtype=jnp.int32) // capacity
    shuffled = jax.vmap(lambda single: jax.random.permutation(single, grouped))(subkeys[:devices])
    device_ids = jnp.arange(devices, dtype=jnp.int32)[:, None]
    if by_branch:
        owners = shuffled * N_SUBTREE + device_ids % N_SUBTREE
    else:
        owners = device_ids // N_SUBTREE * N_SUBTREE + shuffled
    within = jax.random.randint(subkeys[devices], (devices, entries), 0, rows_dev)
    return (owners * rows_dev + within).astype(jnp.int32).reshape(devices * rows_dev, slots)


def draw_leaf_list(key, part):
    key = jax.random.fold_in(key, 11)
    return spread_lists(key, LEAF_DEV, M_LEAF, CAP, False)


def draw_parent_list(key, part):
    key = jax.random.fold_in(key, 23)
    return spread_lists(key, PAR_DEV, M_PAR, CAPP, True)


def plant(drawn, rng, least, top_value):
    longest = drawn.shape.index(max(drawn.shape))
    spots = []
    for shift in (0, 1):
        where = [jax.random.randint(jax.random.fold_in(rng, axis), (), 0, length) for axis, length in enumerate(drawn.shape)]
        where[longest] = (where[longest] + shift) % drawn.shape[longest]
        spots.append(tuple(where))
    return drawn.at[spots[0]].set(least).at[spots[1]].set(top_value)


def shard_levels(own_key, shape, cuts, least, top_value):
    def one(dim, blocks):
        steps = jax.random.uniform(jax.random.fold_in(jax.random.fold_in(own_key, 6), dim), (blocks,), jnp.float32, least / len(cuts), top_value / len(cuts))
        return jnp.repeat(jnp.exp(steps), shape[dim] // blocks).reshape((-1,) + (1,) * (len(shape) - dim - 1))

    level = one(*cuts[0])
    for cut in cuts[1:]:
        level = level * one(*cut)
    return level


def gaussian(key, dims, deviation, reach, cuts=(), kind=jnp.bfloat16):
    values = deviation * jax.random.normal(key, dims, jnp.float32)
    if cuts:
        values = values * shard_levels(key, dims, cuts, -0.22, 0.18)
    return jnp.clip(values, -reach, reach).astype(kind)


def setup_inputs(seed: int = 0) -> dict:
    keys = jax.random.split(jax.random.key(seed), 10)
    vectors = gaussian(keys[0], (NV, NPTS), 1.0, 6.0, ((1, 128),), jnp.float32)
    basis = gaussian(keys[1], (K, NPTS), PTS ** -0.5, 0.75, ((1, 128),), jnp.float32)
    transfer = gaussian(keys[2], (NLEAF, K * K), (CHILD * K) ** -0.5, 0.375, ((0, 128),), jnp.float32)
    leaf_coupling = gaussian(keys[3], (NLEAF, K, M_LEAF * K), (M_LEAF * K) ** -0.5, 0.25, ((0, 128),), jnp.float32)
    leaf_list = draw_leaf_list(jax.random.fold_in(keys[9], 71), 0)
    leaf_mask = plant((jax.random.randint(keys[5], (NLEAF, M_LEAF), 0, 4) < 3).astype(jnp.int32), jax.random.fold_in(keys[5], 1), 0, 1)
    parent_coupling = gaussian(keys[6], (NPAR, K, M_PAR * K), (M_PAR * K) ** -0.5, 0.1875, ((0, 128),), jnp.float32)
    parent_list = draw_parent_list(jax.random.fold_in(keys[9], 71), 0)
    parent_mask = plant((jax.random.randint(keys[8], (NPAR, M_PAR), 0, 4) < 3).astype(jnp.int32), jax.random.fold_in(keys[8], 1), 0, 1)
    return {"vectors": vectors, "basis": basis, "transfer": transfer, "leaf_coupling": leaf_coupling, "leaf_list": leaf_list, "leaf_mask": leaf_mask, "parent_coupling": parent_coupling, "parent_list": parent_list, "parent_mask": parent_mask}


HIGHEST = lax.Precision.HIGHEST


def couple(coefs, lists, masks, coupling):
    count = lists.shape[0]
    slots = lists.shape[1]
    gains = coupling.reshape(count, K, slots, K) * masks.astype(coupling.dtype)[:, None, :, None]
    picked = coefs[lists]
    return jnp.einsum('lamb,lmbv->lav', gains, picked, precision=HIGHEST)


def reference(vectors, basis, transfer, leaf_coupling, leaf_list, leaf_mask, parent_coupling, parent_list, parent_mask):
    leaf_count = leaf_list.shape[0]
    parent_count = parent_list.shape[0]
    points = vectors.reshape(NV, leaf_count, PTS)
    bases = basis.reshape(K, leaf_count, PTS)
    leaf_coef = jnp.einsum('alp,vlp->lav', bases, points, precision=HIGHEST)
    transfers = transfer.reshape(parent_count, CHILD, K, K)
    parent_coef = jnp.einsum('pcab,pcav->pbv', transfers, leaf_coef.reshape(parent_count, CHILD, K, NV), precision=HIGHEST)
    leaf_blocks = leaf_count // LEAF_DEV

    def leaf_block(pieces):
        return couple(leaf_coef, pieces[0], pieces[1], pieces[2])

    leaf_field = lax.map(leaf_block, (leaf_list.reshape(leaf_blocks, LEAF_DEV, M_LEAF), leaf_mask.reshape(leaf_blocks, LEAF_DEV, M_LEAF), leaf_coupling.reshape(leaf_blocks, LEAF_DEV, K, M_LEAF * K)))
    leaf_field = leaf_field.reshape(leaf_count, K, NV)
    parent_blocks = parent_count // PAR_DEV

    def parent_block(pieces):
        return couple(parent_coef, pieces[0], pieces[1], pieces[2])

    parent_field = lax.map(parent_block, (parent_list.reshape(parent_blocks, PAR_DEV, M_PAR), parent_mask.reshape(parent_blocks, PAR_DEV, M_PAR), parent_coupling.reshape(parent_blocks, PAR_DEV, K, M_PAR * K)))
    parent_field = parent_field.reshape(parent_count, K, NV)
    downward = jnp.einsum('pcab,pbv->pcav', transfers, parent_field, precision=HIGHEST)
    total_field = leaf_field + downward.reshape(leaf_count, K, NV)
    result = jnp.einsum('alp,lav->vlp', bases, total_field, precision=HIGHEST)
    return result.reshape(NV, leaf_count * PTS)
```

```python
import functools

import jax
import jax.numpy as jnp
from jax import lax
from jax.experimental import pallas as pl
from jax.experimental.pallas import tpu as pltpu
from jax.sharding import PartitionSpec as P

PTS = 64
K = 32
NV = 64
CHILD = 8
HALF = K // 2
LANES = 2 * NV

HIGHEST = lax.Precision.HIGHEST


def split(x):
    high = x.astype(jnp.bfloat16)
    low = (x - high.astype(jnp.float32)).astype(jnp.bfloat16)
    return high, low


def left_lanes(rows):
    return lax.broadcasted_iota(jnp.int32, (rows, LANES), 1) < NV


def coef_kernel(basis_ref, vectors_ref, out_ref):
    pairs = basis_ref.shape[1] // LANES
    left_v = left_lanes(NV)
    left_h = left_lanes(HALF)
    for pair in range(pairs):
        lanes = slice(pair * LANES, (pair + 1) * LANES)
        basis_high, basis_low = split(basis_ref[:, lanes])
        vec_high, vec_low = split(vectors_ref[:, lanes])
        zero = jnp.zeros_like(vec_high)
        weights = jnp.concatenate(
            [
                jnp.where(left_v, vec_high, zero),
                jnp.where(left_v, zero, vec_high),
                jnp.where(left_v, vec_low, zero),
                jnp.where(left_v, zero, vec_low),
            ],
            axis=0,
        )
        both = lax.dot_general(
            jnp.concatenate([basis_high, basis_low], axis=0),
            weights,
            (((1,), (1,)), ((), ())),
            preferred_element_type=jnp.float32,
        )
        summed = both[:K, :LANES] + (both[:K, LANES:] + both[K:, :LANES])
        upper, lower = summed[:HALF], summed[HALF:]
        out_ref[2 * pair] = jnp.where(left_h, upper, pltpu.roll(lower, NV, 1))
        out_ref[2 * pair + 1] = jnp.where(left_h, pltpu.roll(upper, NV, 1), lower)


def leaf_coefs(basis, vectors, block):
    leaves = basis.shape[1] // PTS
    return pl.pallas_call(
        coef_kernel,
        out_shape=jax.ShapeDtypeStruct((leaves, HALF, LANES), jnp.float32),
        grid=(leaves // block,),
        in_specs=[
            pl.BlockSpec((K, block * PTS), lambda i: (0, i)),
            pl.BlockSpec((NV, block * PTS), lambda i: (0, i)),
        ],
        out_specs=pl.BlockSpec((block, HALF, LANES), lambda i: (i, 0, 0)),
        compiler_params=pltpu.CompilerParams(vmem_limit_bytes=32 * 2**20),
        name="leaf_coef",
    )(basis, vectors)


def field_kernel(slots, where_ref, mask_ref, group_ref, coupling_ref, down_ref, basis_ref, out_ref):
    block = coupling_ref.shape[0]
    first = pl.program_id(0) * block
    left_h = left_lanes(HALF)
    left_k = left_lanes(K)
    left_v = left_lanes(NV)

    def leaf_field(leaf):
        parts = []
        for slot in range(slots):
            entry = (first + leaf) * slots + slot
            picked = group_ref[where_ref[entry]] * mask_ref[entry].astype(jnp.float32)
            high = picked.astype(jnp.bfloat16)
            high32 = high.astype(jnp.float32)
            low = pltpu.roll(picked - high32, NV, 1)
            parts.append(jnp.where(left_h, high32, low).astype(jnp.bfloat16))
            parts.append(jnp.where(left_h, low, high32).astype(jnp.bfloat16))
        both = jnp.dot(
            jnp.concatenate(split(coupling_ref[leaf]), axis=0),
            jnp.concatenate(parts, axis=0),
            preferred_element_type=jnp.float32,
        )
        summed = both[:K] + both[K:]
        return summed + pltpu.roll(summed, NV, 1)

    def one_pair(pair):
        total = jnp.where(left_k, leaf_field(2 * pair), leaf_field(2 * pair + 1)) + down_ref[pair]
        lanes = pl.ds(pl.multiple_of(pair * LANES, LANES), LANES)
        total_high, total_low = split(total)
        basis_high, basis_low = split(basis_ref[:, lanes])
        both = lax.dot_general(
            jnp.concatenate([total_high, total_low, total_high], axis=0),
            jnp.concatenate([basis_high, basis_high, basis_low], axis=0),
            (((0,), (0,)), ((), ())),
            preferred_element_type=jnp.float32,
        )
        out_ref[:, lanes] = jnp.where(left_v, both[:NV], both[NV:])

    @pl.loop(0, block // 4)
    def _(quad):
        one_pair(2 * quad)
        one_pair(2 * quad + 1)


def products(where, mask, group, coupling, down, basis, block):
    leaves, _, width = coupling.shape
    slots = width // K
    smem = pl.BlockSpec(memory_space=pltpu.SMEM)
    return pl.pallas_call(
        functools.partial(field_kernel, slots),
        out_shape=jax.ShapeDtypeStruct((NV, leaves * PTS), jnp.float32),
        grid=(leaves // block,),
        in_specs=[
            smem,
            smem,
            pl.BlockSpec(memory_space=pltpu.VMEM),
            pl.BlockSpec((block, K, width), lambda i: (i, 0, 0)),
            pl.BlockSpec((block // 2, K, LANES), lambda i: (i, 0, 0)),
            pl.BlockSpec((K, block * PTS), lambda i: (0, i)),
        ],
        out_specs=pl.BlockSpec((NV, block * PTS), lambda i: (0, i)),
        compiler_params=pltpu.CompilerParams(vmem_limit_bytes=56 * 2**20),
        name="leaf_field_product",
    )(where, mask, group, coupling, down, basis)


def coupled(coupling, picked, masks):
    count, slots = masks.shape
    masked = picked * masks.reshape(count * slots).astype(jnp.float32)[:, None, None]
    stacked = masked.reshape(count, slots * K, NV)
    return lax.dot_general(
        coupling,
        stacked,
        (((2,), (1,)), ((0,), (0,))),
        precision=HIGHEST,
        preferred_element_type=jnp.float32,
    )


def per_device(
    vectors,
    basis,
    transfer,
    leaf_coupling,
    leaf_list,
    leaf_mask,
    parent_coupling,
    parent_list,
    parent_mask,
):
    leaf_count = leaf_list.shape[0]
    parent_count = parent_list.shape[0]
    subtrees = lax.axis_size("subtree")
    coef = leaf_coefs(basis, vectors, 32)
    group_all = lax.all_gather(coef, "subtree", axis=0, tiled=True)

    natural = coef.reshape(parent_count, CHILD, HALF, 2, NV).transpose(0, 1, 3, 2, 4).reshape(parent_count, CHILD, K, NV)
    transfers = transfer.reshape(parent_count, CHILD, K, K)
    parent_coef = jnp.einsum("pcab,pcav->pbv", transfers, natural, precision=HIGHEST)
    parent_all = lax.all_gather(parent_coef, "branch", axis=0, tiled=True)
    parent_owner = parent_list // parent_count
    position = parent_owner // subtrees * parent_count + parent_list % parent_count
    parent_picked = parent_all[position.reshape(-1)]
    parent_field = coupled(parent_coupling, parent_picked, parent_mask)
    downward = jnp.einsum("pcab,pbv->pcav", transfers, parent_field, precision=HIGHEST)
    down_pairs = downward.reshape(leaf_count // 2, 2, K, NV).transpose(0, 2, 1, 3).reshape(leaf_count // 2, K, LANES)

    where = (leaf_list % (subtrees * leaf_count)).reshape(-1)
    return products(where, leaf_mask.reshape(-1), group_all, leaf_coupling, down_pairs, basis, 16)


def solution(mesh):
    return jax.shard_map(
        per_device,
        mesh=mesh,
        in_specs=(
            P(None, ("branch", "subtree")),
            P(None, ("branch", "subtree")),
            P(("branch", "subtree"), None),
            P(("branch", "subtree"), None, None),
            P(("branch", "subtree"), None),
            P(("branch", "subtree"), None),
            P(("branch", "subtree"), None, None),
            P(("branch", "subtree"), None),
            P(("branch", "subtree"), None),
        ),
        out_specs=P(None, ("branch", "subtree")),
        check_vma=False,
    )
```

```python
import functools

import jax
import jax.numpy as jnp
from jax import lax
from jax.experimental import pallas as pl
from jax.experimental.pallas import tpu as pltpu
from jax.sharding import PartitionSpec as P

PTS = 64
K = 32
NV = 64
CHILD = 8
ROWS = 8
TILE = 16
LANES = 2 * NV
CAP = 64
VMEM_LIMIT = 60 * 2**20
BRIEF = pl.CostEstimate(flops=0, bytes_accessed=0, transcendentals=0)
BRANCHES = 4

def split(x):
    high = x.astype(jnp.bfloat16)
    low = (x - high.astype(jnp.float32)).astype(jnp.bfloat16)
    return high, low


def left_lanes(rows):
    return lax.broadcasted_iota(jnp.int32, (rows, LANES), 1) < NV


def coef_kernel(basis_ref, vectors_ref, coef_ref, pair_ref):
    left_v = left_lanes(NV)
    left_r = left_lanes(ROWS)
    for pair in range(basis_ref.shape[1] // LANES):
        lanes = slice(pair * LANES, (pair + 1) * LANES)
        basis_high, basis_low = split(basis_ref[:, lanes])
        vec_high, vec_low = split(vectors_ref[:, lanes])
        zero = jnp.zeros_like(vec_high)
        weights = jnp.concatenate(
            [
                jnp.where(left_v, vec_high, zero),
                jnp.where(left_v, zero, vec_high),
                jnp.where(left_v, vec_low, zero),
                jnp.where(left_v, zero, vec_low),
            ],
            axis=0,
        )
        both = lax.dot_general(
            jnp.concatenate([basis_high, basis_low], axis=0),
            weights,
            (((1,), (1,)), ((), ())),
            preferred_element_type=jnp.float32,
        )
        summed = both[:K, :LANES] + (both[:K, LANES:] + both[K:, :LANES])
        pair_ref[pair] = summed
        for half in (0, 1):
            first = summed[half * TILE : half * TILE + ROWS]
            second = summed[half * TILE + ROWS : (half + 1) * TILE]
            rows = slice(half * ROWS, (half + 1) * ROWS)
            coef_ref[2 * pair, rows] = jnp.where(left_r, first, pltpu.roll(second, NV, 1))
            coef_ref[2 * pair + 1, rows] = jnp.where(left_r, pltpu.roll(first, NV, 1), second)


def leaf_coefs(basis, vectors, block):
    leaves = basis.shape[1] // PTS
    return pl.pallas_call(
        coef_kernel,
        out_shape=(
            jax.ShapeDtypeStruct((leaves, TILE, LANES), jnp.float32),
            jax.ShapeDtypeStruct((leaves // 2, K, LANES), jnp.float32),
        ),
        grid=(leaves // block,),
        in_specs=[
            pl.BlockSpec((K, block * PTS), lambda i: (0, i)),
            pl.BlockSpec((NV, block * PTS), lambda i: (0, i)),
        ],
        out_specs=(
            pl.BlockSpec((block, TILE, LANES), lambda i: (i, 0, 0)),
            pl.BlockSpec((block // 2, K, LANES), lambda i: (i, 0, 0)),
        ),
        compiler_params=pltpu.CompilerParams(vmem_limit_bytes=VMEM_LIMIT),
        name="leaf_coef",
    )(basis, vectors)


def pick_slot(x, live, left_r):
    x = x * live.astype(jnp.float32)
    high = x.astype(jnp.bfloat16).astype(jnp.float32)
    low = pltpu.roll(x - high, NV, 1)
    return jnp.concatenate([jnp.where(left_r, high, low), jnp.where(left_r, low, high)], axis=0).astype(jnp.bfloat16)


DEPTH = 8
UNROLL = 64


def field_kernel(slots, block, pos_ref, val_ref, group_ref, coupling_ref, down_ref, basis_ref, out_ref, tiles, buf, sem):
    step = pl.program_id(0)
    first = step * block
    left_k, left_r, left_v = left_lanes(K), left_lanes(ROWS), left_lanes(NV)

    @pl.when(step == 0)
    def _():
        leaves = buf.shape[1]
        devices = group_ref.shape[0] // leaves

        def chunk(device):
            at = pl.multiple_of(device * leaves, leaves)
            return pltpu.make_async_copy(
                group_ref.at[pl.ds(at, leaves)], buf.at[lax.rem(device, DEPTH)], sem.at[lax.rem(device, DEPTH)]
            )

        for device in range(DEPTH - 1):
            chunk(device).start()

        @pl.loop(0, devices)
        def _(device):
            @pl.when(device + DEPTH - 1 < devices)
            def _():
                chunk(device + DEPTH - 1).start()

            chunk(device).wait()

            @pl.loop(0, CAP // UNROLL)
            def _(part):
                for n in range(UNROLL):
                    entry = device * CAP + part * UNROLL + n
                    code = val_ref[device, part * UNROLL + n]
                    both = buf[lax.rem(device, DEPTH), code >> 1]
                    tiles[entry, :TILE] = pick_slot(both[:ROWS], code & 1, left_r)
                    tiles[entry, TILE:] = pick_slot(both[ROWS:], code & 1, left_r)

    def leaf_field(leaf):
        parts = [tiles[pos_ref[first + leaf, slot]] for slot in range(slots)]
        both = jnp.dot(
            jnp.concatenate(split(coupling_ref[leaf]), axis=0),
            jnp.concatenate(parts, axis=0),
            preferred_element_type=jnp.float32,
        )
        summed = both[:K] + both[K:]
        return summed + pltpu.roll(summed, NV, 1)

    def pair_total(pair):
        return jnp.where(left_k, leaf_field(2 * pair), leaf_field(2 * pair + 1)) + down_ref[pair]

    def diagonal(x):
        rows = []
        for g in range(4):
            row = [x[:, n * LANES : (n + 1) * LANES] if n == g else jnp.zeros((K, LANES), x.dtype) for n in range(4)]
            rows.append(jnp.concatenate(row, axis=1))
        return jnp.concatenate(rows, axis=0)

    @pl.loop(0, block // 8)
    def _(quad):
        total = jnp.concatenate([pair_total(4 * quad + n) for n in range(4)], axis=0)
        high, low = split(total.T)
        at = pl.multiple_of(quad * 4 * LANES, 4 * LANES)
        basis_high, basis_low = split(basis_ref[:, pl.ds(at, 4 * LANES)])
        spread = diagonal(basis_high)
        both = jnp.dot(
            jnp.concatenate([high, low], axis=1),
            jnp.concatenate([spread, spread], axis=0),
            preferred_element_type=jnp.float32,
        )
        both += jnp.dot(high, diagonal(basis_low), preferred_element_type=jnp.float32)
        for n in range(4):
            square = both[:, n * LANES : (n + 1) * LANES]
            out_ref[:, pl.ds(pl.multiple_of(at + n * LANES, LANES), LANES)] = jnp.where(
                left_v, square[:NV], square[NV:]
            )


def products(pos, codes, group, coupling, down, basis, block):
    leaves, _, width = coupling.shape
    slots = width // K
    smem = pl.BlockSpec(memory_space=pltpu.SMEM)
    return pl.pallas_call(
        functools.partial(field_kernel, slots, block),
        out_shape=jax.ShapeDtypeStruct((NV, leaves * PTS), jnp.float32),
        grid=(leaves // block,),
        in_specs=[
            smem,
            smem,
            pl.BlockSpec(memory_space=pl.ANY),
            pl.BlockSpec((block, K, width), lambda i: (i, 0, 0)),
            pl.BlockSpec((block // 2, K, LANES), lambda i: (i, 0, 0)),
            pl.BlockSpec((K, block * PTS), lambda i: (0, i)),
        ],
        out_specs=pl.BlockSpec((NV, block * PTS), lambda i: (0, i)),
        scratch_shapes=[
            pltpu.VMEM((leaves * slots, K, LANES), jnp.bfloat16),
            pltpu.VMEM((DEPTH, leaves, TILE, LANES), jnp.float32),
            pltpu.SemaphoreType.DMA((DEPTH,)),
        ],
        compiler_params=pltpu.CompilerParams(vmem_limit_bytes=VMEM_LIMIT),
        name="leaf_field_product",
    )(pos, codes, group, coupling, down, basis)


def order_kernel(list_ref, mask_ref, pos_ref, code_ref):
    leaves, slots = list_ref.shape
    devices = code_ref.shape[0]
    names = list_ref[...]
    owner = lax.rem(names // leaves, devices)
    code = (lax.rem(names, leaves) * 2 + mask_ref[...]).astype(jnp.float32)
    row = lax.broadcasted_iota(jnp.int32, (leaves, LANES), 0)
    lane = lax.broadcasted_iota(jnp.int32, (leaves, LANES), 1)
    below = (row > lane).astype(jnp.bfloat16)
    used = jnp.zeros((1, LANES), jnp.float32)
    sorted_codes = jnp.zeros((LANES, LANES), jnp.float32)
    places = jnp.zeros((leaves, LANES), jnp.float32)
    for slot in range(slots):
        named = (owner[:, slot : slot + 1] == lane).astype(jnp.float32)
        before = jnp.dot(below, named.astype(jnp.bfloat16), preferred_element_type=jnp.float32) + used
        used = used + jnp.sum(named, axis=0, keepdims=True)
        index = jnp.sum(named * before, axis=1, keepdims=True)
        rank = jnp.sum(named * lane.astype(jnp.float32), axis=1, keepdims=True)
        places = jnp.where(lane == slot, rank * CAP + index, places)
        spread = (lane.astype(jnp.float32) == index).astype(jnp.bfloat16)
        sorted_codes = sorted_codes + lax.dot_general(
            (named * code[:, slot : slot + 1]).astype(jnp.bfloat16),
            spread,
            (((0,), (0,)), ((), ())),
            preferred_element_type=jnp.float32,
        )
    pos_ref[...] = places[:, :slots].astype(jnp.int32)
    code_ref[...] = sorted_codes[:devices].astype(jnp.int32)


def slot_order(leaf_list, leaf_mask, devices):
    return pl.pallas_call(
        order_kernel,
        out_shape=(
            jax.ShapeDtypeStruct(leaf_list.shape, jnp.int32),
            jax.ShapeDtypeStruct((devices, LANES), jnp.int32),
        ),
        compiler_params=pltpu.CompilerParams(vmem_limit_bytes=VMEM_LIMIT),
        cost_estimate=BRIEF,
        name="slot_order",
    )(leaf_list, leaf_mask)


def parent_coef_kernel(pair_ref, transfer_ref, out_ref):
    left_r = left_lanes(ROWS)
    for parent in range(out_ref.shape[0]):
        blocks = []
        for leaf in range(CHILD):
            pair = parent * CHILD // 2 + leaf // 2
            x = [pair_ref[pair, pl.ds(a4, ROWS, stride=4), :] for a4 in range(4)]
            if leaf % 2 == 0:
                tiles = [jnp.where(left_r, x[n], pltpu.roll(x[n + 1], NV, 1)) for n in (0, 2)]
            else:
                tiles = [jnp.where(left_r, pltpu.roll(x[n], NV, 1), x[n + 1]) for n in (0, 2)]
            blocks.append(jnp.concatenate(tiles, axis=1))
        coef_high, coef_low = split(jnp.concatenate(blocks, axis=0))
        rows = CHILD * ROWS
        high, low = split(transfer_ref[parent * rows : (parent + 1) * rows])
        full = lax.dot_general(
            jnp.concatenate([high, low, high], axis=0),
            jnp.concatenate([coef_high, coef_high, coef_low], axis=0),
            (((0,), (0,)), ((), ())),
            preferred_element_type=jnp.float32,
        )
        even = full[:K, :LANES] + full[2 * K : 3 * K, LANES:]
        odd = full[K : 2 * K, :LANES] + full[3 * K :, LANES:]
        total = even + pltpu.roll(odd, NV, 1)
        for half in (0, 1):
            first = total[half * TILE : half * TILE + ROWS]
            second = total[half * TILE + ROWS : (half + 1) * TILE]
            out_ref[parent, half * ROWS : (half + 1) * ROWS] = jnp.where(left_r, first, pltpu.roll(second, NV, 1))


def parent_coefs(coef_pairs, rows):
    parents = coef_pairs.shape[0] * 2 // CHILD
    return pl.pallas_call(
        parent_coef_kernel,
        out_shape=jax.ShapeDtypeStruct((parents, TILE, LANES), jnp.float32),
        compiler_params=pltpu.CompilerParams(vmem_limit_bytes=VMEM_LIMIT),
        cost_estimate=BRIEF,
        name="parent_coef",
    )(coef_pairs, rows)


def parent_field_kernel(group, list_ref, mask_ref, branch_ref, *refs):
    coef_refs, (coupling_ref, transfer_ref, down_ref, coef_ref) = refs[:BRANCHES], refs[BRANCHES:]
    parents = coef_ref.shape[0] // BRANCHES
    slots = list_ref.shape[1]
    parent = pl.program_id(0)
    left_k, left_r = left_lanes(K), left_lanes(ROWS)

    @pl.when(parent == 0)
    def _():
        for number, ref in enumerate(coef_refs):
            coef_ref[number * parents : (number + 1) * parents] = ref[...]

    parts = []
    for slot in range(slots):
        name = list_ref[parent, slot]
        at = lax.rem(name // group - branch_ref[0] + BRANCHES, BRANCHES) * parents + lax.rem(name, parents)
        both = coef_ref[at]
        live = mask_ref[parent, slot]
        parts += [pick_slot(both[:ROWS], live, left_r), pick_slot(both[ROWS:], live, left_r)]
    both = jnp.dot(
        jnp.concatenate(split(coupling_ref[0]), axis=0),
        jnp.concatenate(parts, axis=0),
        preferred_element_type=jnp.float32,
    )
    summed = both[:K] + both[K:]
    field = summed + pltpu.roll(summed, NV, 1)
    zero = jnp.zeros_like(field)
    left, right = jnp.where(left_k, field, zero), jnp.where(left_k, zero, field)
    spread = jnp.concatenate(
        [
            jnp.concatenate([left, right, zero, zero], axis=0),
            jnp.concatenate([zero, zero, left, right], axis=0),
        ],
        axis=1,
    )
    spread_high, spread_low = split(spread)
    high, low = split(transfer_ref[...])
    full = jnp.dot(
        jnp.concatenate([high, low, high], axis=1),
        jnp.concatenate([spread_high, spread_high, spread_low], axis=0),
        preferred_element_type=jnp.float32,
    )
    for pair in range(CHILD // 2):
        for a4 in range(4):
            lanes = slice(a4 // 2 * LANES, (a4 // 2 + 1) * LANES)
            even = full[2 * pair * ROWS : (2 * pair + 1) * ROWS, lanes]
            odd = full[(2 * pair + 1) * ROWS : (2 * pair + 2) * ROWS, lanes]
            if a4 % 2 == 0:
                odd = pltpu.roll(odd, NV, 1)
            else:
                even = pltpu.roll(even, NV, 1)
            down_ref[pair, pl.ds(a4, ROWS, stride=4), :] = jnp.where(left_r, even, odd)


def downward_pairs(parent_list, parent_mask, branch, group, coef_all, coupling, rows):
    parents, _, width = coupling.shape
    smem = pl.BlockSpec(memory_space=pltpu.SMEM)
    return pl.pallas_call(
        functools.partial(parent_field_kernel, group),
        out_shape=jax.ShapeDtypeStruct((parents * CHILD // 2, K, LANES), jnp.float32),
        grid=(parents,),
        in_specs=[
            smem,
            smem,
            smem,
        ]
        + [pl.BlockSpec(memory_space=pltpu.VMEM)] * BRANCHES
        + [
            pl.BlockSpec((1, K, width), lambda i: (i, 0, 0)),
            pl.BlockSpec((CHILD * ROWS, LANES), lambda i: (i, 0)),
        ],
        out_specs=pl.BlockSpec((CHILD // 2, K, LANES), lambda i: (i, 0, 0)),
        scratch_shapes=[pltpu.VMEM((BRANCHES * parents, TILE, LANES), jnp.float32)],
        compiler_params=pltpu.CompilerParams(vmem_limit_bytes=VMEM_LIMIT),
        cost_estimate=BRIEF,
        name="parent_field",
    )(parent_list, parent_mask, branch, *coef_all, coupling, rows)


def per_device(
    vectors,
    basis,
    transfer,
    leaf_coupling,
    leaf_list,
    leaf_mask,
    parent_coupling,
    parent_list,
    parent_mask,
):
    leaf_count = leaf_list.shape[0]
    parent_count = parent_list.shape[0]
    subtrees = lax.axis_size("subtree")
    branches = lax.axis_size("branch")

    coef, coef_pairs = leaf_coefs(basis, vectors, 32)
    group = lax.all_gather(coef, "subtree", axis=0, tiled=True)
    pos, codes = slot_order(leaf_list, leaf_mask, subtrees)

    rows = transfer.reshape(parent_count * CHILD * ROWS, LANES)
    branch = lax.axis_index("branch").astype(jnp.int32)[None]
    parent_coef = parent_coefs(coef_pairs, rows)
    coef_all = [parent_coef] + [
        lax.ppermute(parent_coef, "branch", [(i, (i - by) % branches) for i in range(branches)])
        for by in range(1, branches)
    ]
    down = downward_pairs(parent_list, parent_mask, branch, parent_count * subtrees, coef_all, parent_coupling, rows)
    return products(pos, codes, group, leaf_coupling, down, basis, 32)


def solution(mesh):
    return jax.shard_map(
        per_device,
        mesh=mesh,
        in_specs=(
            P(None, ("branch", "subtree")),
            P(None, ("branch", "subtree")),
            P(("branch", "subtree"), None),
            P(("branch", "subtree"), None, None),
            P(("branch", "subtree"), None),
            P(("branch", "subtree"), None),
            P(("branch", "subtree"), None, None),
            P(("branch", "subtree"), None),
            P(("branch", "subtree"), None),
        ),
        out_specs=P(None, ("branch", "subtree")),
        check_vma=False,
    )
```

```python
import functools

import jax
import jax.numpy as jnp
from jax import lax
from jax.experimental import pallas as pl
from jax.experimental.pallas import tpu as pltpu
from jax.sharding import PartitionSpec as P

PTS = 64
K = 32
NV = 64
CHILD = 8
ROWS = 8
TILE = 16
LANES = 2 * NV
CAP = 64
VMEM_LIMIT = 60 * 2**20
BRIEF = pl.CostEstimate(flops=0, bytes_accessed=0, transcendentals=0)
BRANCHES = 4

def split(x):
    high = x.astype(jnp.bfloat16)
    low = (x - high.astype(jnp.float32)).astype(jnp.bfloat16)
    return high, low


def left_lanes(rows):
    return lax.broadcasted_iota(jnp.int32, (rows, LANES), 1) < NV


def coef_kernel(basis_ref, vectors_ref, coef_ref, pair_ref):
    left_k = left_lanes(K)
    left_r = left_lanes(ROWS)
    for pair in range(basis_ref.shape[1] // LANES):
        lanes = slice(pair * LANES, (pair + 1) * LANES)
        rows = []
        for part in split(basis_ref[:, lanes]):
            zero = jnp.zeros_like(part)
            rows += [jnp.where(left_k, part, zero), jnp.where(left_k, zero, part)]
        both = lax.dot_general(
            jnp.concatenate(rows, axis=0),
            jnp.concatenate(split(vectors_ref[:, lanes]), axis=0),
            (((1,), (1,)), ((), ())),
            preferred_element_type=jnp.float32,
        )
        even, odd = both[:K] + both[2 * K : 3 * K], both[K : 2 * K] + both[3 * K :]
        even, odd = even + pltpu.roll(even, NV, 1), odd + pltpu.roll(odd, NV, 1)
        pair_ref[pair] = jnp.where(left_k, even, odd)
        for half in (0, 1):
            first = slice(half * TILE, half * TILE + ROWS)
            second = slice(half * TILE + ROWS, (half + 1) * TILE)
            rows = slice(half * ROWS, (half + 1) * ROWS)
            coef_ref[2 * pair, rows] = jnp.where(left_r, even[first], even[second])
            coef_ref[2 * pair + 1, rows] = jnp.where(left_r, odd[first], odd[second])


def leaf_coefs(basis, vectors, block):
    leaves = basis.shape[1] // PTS
    return pl.pallas_call(
        coef_kernel,
        out_shape=(
            jax.ShapeDtypeStruct((leaves, TILE, LANES), jnp.float32),
            jax.ShapeDtypeStruct((leaves // 2, K, LANES), jnp.float32),
        ),
        grid=(leaves // block,),
        in_specs=[
            pl.BlockSpec((K, block * PTS), lambda i: (0, i)),
            pl.BlockSpec((NV, block * PTS), lambda i: (0, i)),
        ],
        out_specs=(
            pl.BlockSpec((block, TILE, LANES), lambda i: (i, 0, 0)),
            pl.BlockSpec((block // 2, K, LANES), lambda i: (i, 0, 0)),
        ),
        compiler_params=pltpu.CompilerParams(vmem_limit_bytes=VMEM_LIMIT),
        name="leaf_coef",
    )(basis, vectors)


def pick_slot(x, live, left_r):
    x = x * live.astype(jnp.float32)
    high = x.astype(jnp.bfloat16).astype(jnp.float32)
    low = pltpu.roll(x - high, NV, 1)
    return jnp.concatenate([jnp.where(left_r, high, low), jnp.where(left_r, low, high)], axis=0).astype(jnp.bfloat16)


DEPTH = 8
UNROLL = 64


def field_kernel(slots, block, pos_ref, val_ref, group_ref, coupling_ref, down_ref, basis_ref, out_ref, tiles, buf, totals, sem):
    step = pl.program_id(0)
    first = step * block
    left_k, left_r, left_v = left_lanes(K), left_lanes(ROWS), left_lanes(NV)

    @pl.when(step == 0)
    def _():
        leaves = buf.shape[1]
        devices = group_ref.shape[0] // leaves

        def chunk(device):
            at = pl.multiple_of(device * leaves, leaves)
            return pltpu.make_async_copy(
                group_ref.at[pl.ds(at, leaves)], buf.at[lax.rem(device, DEPTH)], sem.at[lax.rem(device, DEPTH)]
            )

        for device in range(DEPTH - 1):
            chunk(device).start()

        @pl.loop(0, devices)
        def _(device):
            @pl.when(device + DEPTH - 1 < devices)
            def _():
                chunk(device + DEPTH - 1).start()

            chunk(device).wait()

            @pl.loop(0, CAP // UNROLL)
            def _(part):
                for n in range(UNROLL):
                    entry = device * CAP + part * UNROLL + n
                    code = val_ref[device, part * UNROLL + n]
                    both = buf[lax.rem(device, DEPTH), code >> 1]
                    tiles[entry, :TILE] = pick_slot(both[:ROWS], code & 1, left_r)
                    tiles[entry, TILE:] = pick_slot(both[ROWS:], code & 1, left_r)

    def leaf_field(leaf):
        parts = [tiles[pos_ref[first + leaf, slot]] for slot in range(slots)]
        both = jnp.dot(
            jnp.concatenate(split(coupling_ref[leaf]), axis=0),
            jnp.concatenate(parts, axis=0),
            preferred_element_type=jnp.float32,
        )
        summed = both[:K] + both[K:]
        return summed + pltpu.roll(summed, NV, 1)

    def pair_total(pair):
        return jnp.where(left_k, leaf_field(2 * pair), leaf_field(2 * pair + 1)) + down_ref[pair]

    def diagonal(x):
        rows = []
        for g in range(4):
            row = [x[:, n * LANES : (n + 1) * LANES] if n == g else jnp.zeros((K, LANES), x.dtype) for n in range(4)]
            rows.append(jnp.concatenate(row, axis=1))
        return jnp.concatenate(rows, axis=0)

    def product(quad, total):
        high, low = split(total.T)
        at = pl.multiple_of(quad * 4 * LANES, 4 * LANES)
        basis_high, basis_low = split(basis_ref[:, pl.ds(at, 4 * LANES)])
        spread = diagonal(basis_high)
        both = jnp.dot(
            jnp.concatenate([high, low], axis=1),
            jnp.concatenate([spread, spread], axis=0),
            preferred_element_type=jnp.float32,
        )
        both += jnp.dot(high, diagonal(basis_low), preferred_element_type=jnp.float32)
        for n in range(4):
            square = both[:, n * LANES : (n + 1) * LANES]
            out_ref[:, pl.ds(pl.multiple_of(at + n * LANES, LANES), LANES)] = jnp.where(
                left_v, square[:NV], square[NV:]
            )

    quads = block // 8
    totals_first = step * quads

    @pl.when(step == 0)
    def _():
        totals[...] = jnp.zeros_like(totals)

    @pl.loop(0, quads // 2)
    def _(turn):
        for n in (0, 1):
            quad = totals_first + 2 * turn + n
            before = totals[1 - n]
            for pair in range(4):
                totals[n, pair * K : (pair + 1) * K] = pair_total(8 * turn + 4 * n + pair)
            product(jnp.maximum(quad - 1, 0), before)

    @pl.when(step == pl.num_programs(0) - 1)
    def _():
        product(totals_first + quads - 1, totals[1])


def products(pos, codes, group, coupling, down, basis, block):
    leaves, _, width = coupling.shape
    slots = width // K
    smem = pl.BlockSpec(memory_space=pltpu.SMEM)
    return pl.pallas_call(
        functools.partial(field_kernel, slots, block),
        out_shape=jax.ShapeDtypeStruct((NV, leaves * PTS), jnp.float32),
        grid=(leaves // block,),
        in_specs=[
            smem,
            smem,
            pl.BlockSpec(memory_space=pl.ANY),
            pl.BlockSpec((block, K, width), lambda i: (i, 0, 0)),
            pl.BlockSpec((block // 2, K, LANES), lambda i: (i, 0, 0)),
            pl.BlockSpec((K, leaves * PTS), lambda i: (0, 0)),
        ],
        out_specs=pl.BlockSpec((NV, leaves * PTS), lambda i: (0, 0)),
        scratch_shapes=[
            pltpu.VMEM((leaves * slots, K, LANES), jnp.bfloat16),
            pltpu.VMEM((DEPTH, leaves, TILE, LANES), jnp.float32),
            pltpu.VMEM((2, 4 * K, LANES), jnp.float32),
            pltpu.SemaphoreType.DMA((DEPTH,)),
        ],
        compiler_params=pltpu.CompilerParams(vmem_limit_bytes=VMEM_LIMIT),
        name="leaf_field_product",
    )(pos, codes, group, coupling, down, basis)


def order_kernel(list_ref, mask_ref, pos_ref, code_ref):
    leaves, slots = list_ref.shape
    devices = code_ref.shape[0]
    names = list_ref[...]
    owner = lax.rem(names // leaves, devices)
    code = (lax.rem(names, leaves) * 2 + mask_ref[...]).astype(jnp.float32)
    row = lax.broadcasted_iota(jnp.int32, (leaves, LANES), 0)
    lane = lax.broadcasted_iota(jnp.int32, (leaves, LANES), 1)
    below = (row > lane).astype(jnp.bfloat16)
    used = jnp.zeros((1, LANES), jnp.float32)
    sorted_codes = jnp.zeros((LANES, LANES), jnp.float32)
    places = jnp.zeros((leaves, LANES), jnp.float32)
    for slot in range(slots):
        named = (owner[:, slot : slot + 1] == lane).astype(jnp.float32)
        before = jnp.dot(below, named.astype(jnp.bfloat16), preferred_element_type=jnp.float32) + used
        used = used + jnp.sum(named, axis=0, keepdims=True)
        index = jnp.sum(named * before, axis=1, keepdims=True)
        rank = jnp.sum(named * lane.astype(jnp.float32), axis=1, keepdims=True)
        places = jnp.where(lane == slot, rank * CAP + index, places)
        spread = (lane.astype(jnp.float32) == index).astype(jnp.bfloat16)
        sorted_codes = sorted_codes + lax.dot_general(
            (named * code[:, slot : slot + 1]).astype(jnp.bfloat16),
            spread,
            (((0,), (0,)), ((), ())),
            preferred_element_type=jnp.float32,
        )
    pos_ref[...] = places[:, :slots].astype(jnp.int32)
    code_ref[...] = sorted_codes[:devices].astype(jnp.int32)


def slot_order(leaf_list, leaf_mask, devices):
    return pl.pallas_call(
        order_kernel,
        out_shape=(
            jax.ShapeDtypeStruct(leaf_list.shape, jnp.int32),
            jax.ShapeDtypeStruct((devices, LANES), jnp.int32),
        ),
        compiler_params=pltpu.CompilerParams(vmem_limit_bytes=VMEM_LIMIT),
        cost_estimate=BRIEF,
        name="slot_order",
    )(leaf_list, leaf_mask)


def parent_coef_kernel(pair_ref, transfer_ref, out_ref):
    left_r = left_lanes(ROWS)
    for parent in range(out_ref.shape[0]):
        blocks = []
        for leaf in range(CHILD):
            pair = parent * CHILD // 2 + leaf // 2
            x = [pair_ref[pair, pl.ds(a4, ROWS, stride=4), :] for a4 in range(4)]
            if leaf % 2 == 0:
                tiles = [jnp.where(left_r, x[n], pltpu.roll(x[n + 1], NV, 1)) for n in (0, 2)]
            else:
                tiles = [jnp.where(left_r, pltpu.roll(x[n], NV, 1), x[n + 1]) for n in (0, 2)]
            blocks.append(jnp.concatenate(tiles, axis=1))
        coef_high, coef_low = split(jnp.concatenate(blocks, axis=0))
        rows = CHILD * ROWS
        high, low = split(transfer_ref[parent * rows : (parent + 1) * rows])
        full = lax.dot_general(
            jnp.concatenate([high, low, high], axis=0),
            jnp.concatenate([coef_high, coef_high, coef_low], axis=0),
            (((0,), (0,)), ((), ())),
            preferred_element_type=jnp.float32,
        )
        even = full[:K, :LANES] + full[2 * K : 3 * K, LANES:]
        odd = full[K : 2 * K, :LANES] + full[3 * K :, LANES:]
        total = even + pltpu.roll(odd, NV, 1)
        for half in (0, 1):
            first = total[half * TILE : half * TILE + ROWS]
            second = total[half * TILE + ROWS : (half + 1) * TILE]
            out_ref[parent, half * ROWS : (half + 1) * ROWS] = jnp.where(left_r, first, pltpu.roll(second, NV, 1))


def parent_coefs(coef_pairs, rows):
    parents = coef_pairs.shape[0] * 2 // CHILD
    return pl.pallas_call(
        parent_coef_kernel,
        out_shape=jax.ShapeDtypeStruct((parents, TILE, LANES), jnp.float32),
        compiler_params=pltpu.CompilerParams(vmem_limit_bytes=VMEM_LIMIT),
        cost_estimate=BRIEF,
        name="parent_coef",
    )(coef_pairs, rows)


def parent_field_kernel(group, list_ref, mask_ref, branch_ref, *refs):
    coef_refs, (coupling_ref, transfer_ref, down_ref, coef_ref) = refs[:BRANCHES], refs[BRANCHES:]
    parents = coef_ref.shape[0] // BRANCHES
    slots = list_ref.shape[1]
    parent = pl.program_id(0)
    left_k, left_r = left_lanes(K), left_lanes(ROWS)

    @pl.when(parent == 0)
    def _():
        for number, ref in enumerate(coef_refs):
            coef_ref[number * parents : (number + 1) * parents] = ref[...]

    parts = []
    for slot in range(slots):
        name = list_ref[parent, slot]
        at = lax.rem(name // group - branch_ref[0] + BRANCHES, BRANCHES) * parents + lax.rem(name, parents)
        both = coef_ref[at]
        live = mask_ref[parent, slot]
        parts += [pick_slot(both[:ROWS], live, left_r), pick_slot(both[ROWS:], live, left_r)]
    both = jnp.dot(
        jnp.concatenate(split(coupling_ref[0]), axis=0),
        jnp.concatenate(parts, axis=0),
        preferred_element_type=jnp.float32,
    )
    summed = both[:K] + both[K:]
    field = summed + pltpu.roll(summed, NV, 1)
    zero = jnp.zeros_like(field)
    left, right = jnp.where(left_k, field, zero), jnp.where(left_k, zero, field)
    spread = jnp.concatenate(
        [
            jnp.concatenate([left, right, zero, zero], axis=0),
            jnp.concatenate([zero, zero, left, right], axis=0),
        ],
        axis=1,
    )
    spread_high, spread_low = split(spread)
    high, low = split(transfer_ref[...])
    full = jnp.dot(
        jnp.concatenate([high, low, high], axis=1),
        jnp.concatenate([spread_high, spread_high, spread_low], axis=0),
        preferred_element_type=jnp.float32,
    )
    for pair in range(CHILD // 2):
        for a4 in range(4):
            lanes = slice(a4 // 2 * LANES, (a4 // 2 + 1) * LANES)
            even = full[2 * pair * ROWS : (2 * pair + 1) * ROWS, lanes]
            odd = full[(2 * pair + 1) * ROWS : (2 * pair + 2) * ROWS, lanes]
            if a4 % 2 == 0:
                odd = pltpu.roll(odd, NV, 1)
            else:
                even = pltpu.roll(even, NV, 1)
            down_ref[pair, pl.ds(a4, ROWS, stride=4), :] = jnp.where(left_r, even, odd)


def downward_pairs(parent_list, parent_mask, branch, group, coef_all, coupling, rows):
    parents, _, width = coupling.shape
    smem = pl.BlockSpec(memory_space=pltpu.SMEM)
    return pl.pallas_call(
        functools.partial(parent_field_kernel, group),
        out_shape=jax.ShapeDtypeStruct((parents * CHILD // 2, K, LANES), jnp.float32),
        grid=(parents,),
        in_specs=[
            smem,
            smem,
            smem,
        ]
        + [pl.BlockSpec(memory_space=pltpu.VMEM)] * BRANCHES
        + [
            pl.BlockSpec((1, K, width), lambda i: (i, 0, 0)),
            pl.BlockSpec((CHILD * ROWS, LANES), lambda i: (i, 0)),
        ],
        out_specs=pl.BlockSpec((CHILD // 2, K, LANES), lambda i: (i, 0, 0)),
        scratch_shapes=[pltpu.VMEM((BRANCHES * parents, TILE, LANES), jnp.float32)],
        compiler_params=pltpu.CompilerParams(vmem_limit_bytes=VMEM_LIMIT),
        cost_estimate=BRIEF,
        name="parent_field",
    )(parent_list, parent_mask, branch, *coef_all, coupling, rows)


def per_device(
    vectors,
    basis,
    transfer,
    leaf_coupling,
    leaf_list,
    leaf_mask,
    parent_coupling,
    parent_list,
    parent_mask,
):
    leaf_count = leaf_list.shape[0]
    parent_count = parent_list.shape[0]
    subtrees = lax.axis_size("subtree")
    branches = lax.axis_size("branch")

    coef, coef_pairs = leaf_coefs(basis, vectors, 64)
    group = lax.all_gather(coef, "subtree", axis=0, tiled=True)
    pos, codes = slot_order(leaf_list, leaf_mask, subtrees)

    rows = transfer.reshape(parent_count * CHILD * ROWS, LANES)
    branch = lax.axis_index("branch").astype(jnp.int32)[None]
    parent_coef = parent_coefs(coef_pairs, rows)
    coef_all = [parent_coef] + [
        lax.ppermute(parent_coef, "branch", [(i, (i - by) % branches) for i in range(branches)])
        for by in range(1, branches)
    ]
    down = downward_pairs(parent_list, parent_mask, branch, parent_count * subtrees, coef_all, parent_coupling, rows)
    return products(pos, codes, group, leaf_coupling, down, basis, 32)


def solution(mesh):
    return jax.shard_map(
        per_device,
        mesh=mesh,
        in_specs=(
            P(None, ("branch", "subtree")),
            P(None, ("branch", "subtree")),
            P(("branch", "subtree"), None),
            P(("branch", "subtree"), None, None),
            P(("branch", "subtree"), None),
            P(("branch", "subtree"), None),
            P(("branch", "subtree"), None, None),
            P(("branch", "subtree"), None),
            P(("branch", "subtree"), None),
        ),
        out_specs=P(None, ("branch", "subtree")),
        check_vma=False,
    )
```

```python
import functools

import jax
import jax.numpy as jnp
from jax import lax
from jax.experimental import pallas as pl
from jax.experimental.pallas import tpu as pltpu
from jax.sharding import PartitionSpec as P

PTS = 64
K = 32
NV = 64
CHILD = 8
ROWS = 8
TILE = 16
LANES = 2 * NV
CAP = 64
SIDE = 4
QUARTERS = 4
BRANCHES = 4

BRIEF = pl.CostEstimate(flops=0, bytes_accessed=0, transcendentals=0)
FINAL_LIMIT = 44 * 2**20
SMALL_LIMIT = 20 * 2**20
LONG = pl.CostEstimate(flops=10**11, bytes_accessed=10**9, transcendentals=0)

CROSS = [(0, 0)]
STEP1 = [(1, 0), (3, 0), (0, 1), (0, 3)]
STEP2 = [(1, 1), (1, 3), (3, 1), (3, 3), (2, 0), (0, 2)]
STEP3 = [(2, 1), (2, 3), (1, 2), (3, 2)]
STEP4 = [(2, 2)]
STAGES = [CROSS + STEP1, STEP2, STEP3, STEP4]
ORDER = [(dy, dz, flip) for stage in STAGES for flip in (0, 1) for dy, dz in stage]


def split(x):
    high = x.astype(jnp.bfloat16)
    low = (x - high.astype(jnp.float32)).astype(jnp.bfloat16)
    return high, low


def left_lanes(rows):
    return lax.broadcasted_iota(jnp.int32, (rows, LANES), 1) < NV


def coef_kernel(basis_ref, vectors_ref, coef_ref, pair_ref):
    left_k = left_lanes(K)
    left_r = left_lanes(ROWS)
    for pair in range(basis_ref.shape[1] // LANES):
        lanes = slice(pair * LANES, (pair + 1) * LANES)
        rows = []
        for part in split(basis_ref[:, lanes]):
            zero = jnp.zeros_like(part)
            rows += [jnp.where(left_k, part, zero), jnp.where(left_k, zero, part)]
        both = lax.dot_general(
            jnp.concatenate(rows, axis=0),
            jnp.concatenate(split(vectors_ref[:, lanes]), axis=0),
            (((1,), (1,)), ((), ())),
            preferred_element_type=jnp.float32,
        )
        even, odd = both[:K] + both[2 * K : 3 * K], both[K : 2 * K] + both[3 * K :]
        even, odd = even + pltpu.roll(even, NV, 1), odd + pltpu.roll(odd, NV, 1)
        pair_ref[pair] = jnp.where(left_k, even, odd)
        for half in (0, 1):
            first = slice(half * TILE, half * TILE + ROWS)
            second = slice(half * TILE + ROWS, (half + 1) * TILE)
            rows = slice(half * ROWS, (half + 1) * ROWS)
            coef_ref[2 * pair, rows] = jnp.where(left_r, even[first], even[second])
            coef_ref[2 * pair + 1, rows] = jnp.where(left_r, odd[first], odd[second])


def leaf_coefs(basis, vectors, block):
    leaves = basis.shape[1] // PTS
    return pl.pallas_call(
        coef_kernel,
        out_shape=(
            jax.ShapeDtypeStruct((leaves, TILE, LANES), jnp.float32),
            jax.ShapeDtypeStruct((leaves // 2, K, LANES), jnp.float32),
        ),
        grid=(leaves // block,),
        in_specs=[
            pl.BlockSpec((K, block * PTS), lambda i: (0, i)),
            pl.BlockSpec((NV, block * PTS), lambda i: (0, i)),
        ],
        out_specs=(
            pl.BlockSpec((block, TILE, LANES), lambda i: (i, 0, 0)),
            pl.BlockSpec((block // 2, K, LANES), lambda i: (i, 0, 0)),
        ),
        compiler_params=pltpu.CompilerParams(vmem_limit_bytes=SMALL_LIMIT),
        name="leaf_coef",
    )(basis, vectors)


def pick_slot(x, live, left_r):
    x = x * live.astype(jnp.float32)
    high = x.astype(jnp.bfloat16).astype(jnp.float32)
    low = pltpu.roll(x - high, NV, 1)
    return jnp.concatenate([jnp.where(left_r, high, low), jnp.where(left_r, low, high)], axis=0).astype(jnp.bfloat16)


def pick_kernel(plan, first, code_ref, *refs):
    sources, out_ref, held, sem = refs[:-3], refs[-3], refs[-2], refs[-1]
    step = pl.program_id(0)
    left_r = left_lanes(ROWS)

    @pl.when(step == 0)
    def _():
        for device, source, start, target, count in plan:
            pltpu.make_async_copy(
                sources[source].at[pl.ds(start, count)],
                held.at[device, pl.ds(target, count)],
                sem.at[device],
            ).start()

    pltpu.make_async_copy(held.at[step], held.at[step], sem.at[step]).wait()

    @pl.loop(0, CAP // 32)
    def _(part):
        for n in range(32):
            slot = part * 32 + n
            code = code_ref[first + step, slot]
            both = held[step, code >> 1]
            out_ref[slot, :TILE] = pick_slot(both[:ROWS], code & 1, left_r)
            out_ref[slot, TILE:] = pick_slot(both[ROWS:], code & 1, left_r)


def picked_slots(devices, codes, pieces, unit, leaves):
    first = ORDER.index(devices[0])
    arrays, plan = [], []
    for device, key in enumerate(devices):
        for quarter in range(QUARTERS):
            piece, at = next((p, p[1].index(key + (quarter,))) for p in pieces if key + (quarter,) in p[1])
            index = next((i for i, a in enumerate(arrays) if a is piece[0]), None)
            if index is None:
                index = len(arrays)
                arrays.append(piece[0])
            last = plan[-1] if plan else None
            if last and last[0] == device and last[1] == index and last[2] + last[4] == at * unit:
                plan[-1] = last[:4] + (last[4] + unit,)
            else:
                plan.append((device, index, at * unit, quarter * unit, unit))
    count = len(devices)
    return pl.pallas_call(
        functools.partial(pick_kernel, plan, first),
        out_shape=jax.ShapeDtypeStruct((count * CAP, K, LANES), jnp.bfloat16),
        grid=(count,),
        in_specs=[pl.BlockSpec(memory_space=pltpu.SMEM)] + [pl.BlockSpec(memory_space=pl.ANY)] * len(arrays),
        out_specs=pl.BlockSpec((CAP, K, LANES), lambda i: (i, 0, 0)),
        scratch_shapes=[
            pltpu.VMEM((count, leaves, TILE, LANES), jnp.float32),
            pltpu.SemaphoreType.DMA((count,)),
        ],
        compiler_params=pltpu.CompilerParams(vmem_limit_bytes=SMALL_LIMIT),
        cost_estimate=BRIEF,
        name="pick",
    )(codes, *arrays)


def arrival_plan(devices, pieces, unit):
    arrays, plan = [], []
    for rank, key in enumerate(devices):
        for quarter in range(QUARTERS):
            piece, at = next((p, p[1].index(key + (quarter,))) for p in pieces if key + (quarter,) in p[1])
            index = next((i for i, a in enumerate(arrays) if a is piece[0]), None)
            if index is None:
                index = len(arrays)
                arrays.append(piece[0])
            last = plan[-1] if plan else None
            if last and last[:2] == (rank, index) and last[2] + last[4] == at * unit:
                plan[-1] = last[:4] + (last[4] + unit,)
            else:
                plan.append((rank, index, at * unit, quarter * unit, unit))
    return arrays, plan


def field_kernel(slots, block, plan, ready, count, pos_ref, code_ref, *refs):
    pieces, sources = refs[:ready], refs[ready : ready + count]
    coupling_ref, down_ref, basis_ref, out_ref, tiles, held, totals, sem, held_sem = refs[ready + count :]
    step = pl.program_id(0)
    first = step * block
    left_k, left_r, left_v = left_lanes(K), left_lanes(ROWS), left_lanes(NV)

    @pl.when(step == 0)
    def _():
        for device, source, start, target, size in plan:
            pltpu.make_async_copy(
                sources[source].at[pl.ds(start, size)], held.at[device, pl.ds(target, size)], held_sem.at[device]
            ).start()
        copies, at = [], 0
        for piece in pieces:
            copies.append(pltpu.make_async_copy(piece, tiles.at[pl.ds(at, piece.shape[0])], sem.at[len(copies)]))
            at += piece.shape[0]
        for copy in copies:
            copy.start()
        early = at // CAP

        @pl.loop(0, held.shape[0])
        def _(device):
            pltpu.make_async_copy(held.at[device], held.at[device], held_sem.at[device]).wait()
            for slot in range(CAP):
                code = code_ref[early + device, slot]
                both = held[device, code >> 1]
                place = (early + device) * CAP + slot
                tiles[place, :TILE] = pick_slot(both[:ROWS], code & 1, left_r)
                tiles[place, TILE:] = pick_slot(both[ROWS:], code & 1, left_r)

        for copy in copies:
            copy.wait()

    def leaf_field(leaf):
        parts = [tiles[pos_ref[first + leaf, slot]] for slot in range(slots)]
        both = jnp.dot(
            jnp.concatenate(split(coupling_ref[leaf]), axis=0),
            jnp.concatenate(parts, axis=0),
            preferred_element_type=jnp.float32,
        )
        summed = both[:K] + both[K:]
        return summed + pltpu.roll(summed, NV, 1)

    def pair_total(pair):
        return jnp.where(left_k, leaf_field(2 * pair), leaf_field(2 * pair + 1)) + down_ref[pair]

    def diagonal(x):
        rows = []
        for g in range(4):
            row = [x[:, n * LANES : (n + 1) * LANES] if n == g else jnp.zeros((K, LANES), x.dtype) for n in range(4)]
            rows.append(jnp.concatenate(row, axis=1))
        return jnp.concatenate(rows, axis=0)

    def product(quad, total):
        high, low = split(total.T)
        at = pl.multiple_of(quad * 4 * LANES, 4 * LANES)
        basis_high, basis_low = split(basis_ref[:, pl.ds(at, 4 * LANES)])
        spread = diagonal(basis_high)
        both = jnp.dot(
            jnp.concatenate([high, low], axis=1),
            jnp.concatenate([spread, spread], axis=0),
            preferred_element_type=jnp.float32,
        )
        both += jnp.dot(high, diagonal(basis_low), preferred_element_type=jnp.float32)
        for n in range(4):
            square = both[:, n * LANES : (n + 1) * LANES]
            out_ref[:, pl.ds(pl.multiple_of(at + n * LANES, LANES), LANES)] = jnp.where(
                left_v, square[:NV], square[NV:]
            )

    quads = block // 8
    totals_first = step * quads

    @pl.when(step == 0)
    def _():
        totals[...] = jnp.zeros_like(totals)

    @pl.loop(0, quads // 2)
    def _(turn):
        for n in (0, 1):
            quad = totals_first + 2 * turn + n
            before = totals[1 - n]
            for pair in range(4):
                totals[n, pair * K : (pair + 1) * K] = pair_total(8 * turn + 4 * n + pair)
            product(jnp.maximum(quad - 1, 0), before)

    @pl.when(step == pl.num_programs(0) - 1)
    def _():
        product(totals_first + quads - 1, totals[1])


def products(pos, codes, tiles, late, pieces, coupling, down, basis, block):
    leaves, _, width = coupling.shape
    slots = width // K
    arrays, plan = arrival_plan(late, pieces, leaves // QUARTERS)
    smem, hbm = pl.BlockSpec(memory_space=pltpu.SMEM), pl.BlockSpec(memory_space=pl.ANY)
    return pl.pallas_call(
        functools.partial(field_kernel, slots, block, plan, len(tiles), len(arrays)),
        out_shape=jax.ShapeDtypeStruct((NV, leaves * PTS), jnp.float32),
        grid=(leaves // block,),
        in_specs=[smem, smem]
        + [hbm] * (len(tiles) + len(arrays))
        + [
            pl.BlockSpec((block, K, width), lambda i: (i, 0, 0)),
            pl.BlockSpec((block // 2, K, LANES), lambda i: (i, 0, 0)),
            pl.BlockSpec((K, leaves * PTS), lambda i: (0, 0)),
        ],
        out_specs=pl.BlockSpec((NV, leaves * PTS), lambda i: (0, 0)),
        scratch_shapes=[
            pltpu.VMEM((leaves * slots, K, LANES), jnp.bfloat16),
            pltpu.VMEM((len(late), leaves, TILE, LANES), jnp.float32),
            pltpu.VMEM((2, 4 * K, LANES), jnp.float32),
            pltpu.SemaphoreType.DMA((len(tiles),)),
            pltpu.SemaphoreType.DMA((len(late),)),
        ],
        compiler_params=pltpu.CompilerParams(vmem_limit_bytes=FINAL_LIMIT),
        cost_estimate=BRIEF,
        name="leaf_field_product",
    )(pos, codes, *tiles, *arrays, coupling, down, basis)


def subtree_index(dy, dz, flip, z, y, core):
    return (z + dz) % SIDE * (2 * SIDE) + (y + dy) % SIDE * 2 + (core + flip) % 2


def moved(piece, axis, by, send):
    array, segs = piece
    perm, out = [], []
    for z in range(SIDE):
        for y in range(SIDE):
            for core in range(2):
                step = {"y": (by, 0, 0), "z": (0, by, 0), "core": (0, 0, 1)}[axis]
                perm.append((subtree_index(0, 0, 0, z, y, core), subtree_index(*step, z, y, core)))
    for dy, dz, flip, quarter in segs:
        if axis == "y":
            out.append(((dy - by) % SIDE, dz, flip, quarter))
        elif axis == "z":
            out.append((dy, (dz - by) % SIDE, flip, quarter))
        else:
            out.append((dy, dz, 1 - flip, quarter))
    return send(array, "subtree", perm), out


class Turns:
    def __init__(self):
        self.last = None

    def __call__(self, array, axis, perm, after=()):
        if self.last is not None:
            array, _ = lax.optimization_barrier((array, (self.last, after)))
        self.last = lax.ppermute(array, axis, perm)
        return self.last


def pack_kernel(plan, count, *refs):
    sources, targets, (held, read_sem, write_sem) = refs[:count], refs[count:-3], refs[-3:]
    reads, writes, base = [], [], 0
    for number, (source, start, target, at, size) in enumerate(plan):
        place = held.at[pl.ds(base, size)]
        reads.append(pltpu.make_async_copy(sources[source].at[pl.ds(start, size)], place, read_sem.at[number]))
        writes.append(pltpu.make_async_copy(place, targets[target].at[pl.ds(at, size)], write_sem.at[number]))
        base += size
    for read in reads:
        read.start()
    for read, write in zip(reads, writes, strict=True):
        read.wait()
        write.start()
    for write in writes:
        write.wait()


def packed(pieces, wanted, unit, cost=BRIEF):
    arrays, plan = [], []
    for target, keys in enumerate(wanted):
        for at, key in enumerate(keys):
            piece = next(p for p in pieces if key in p[1])
            source = next((i for i, a in enumerate(arrays) if a is piece[0]), None)
            if source is None:
                source = len(arrays)
                arrays.append(piece[0])
            start = piece[1].index(key) * unit
            last = plan[-1] if plan else None
            if last and last[0] == source and last[2] == target and last[1] + last[4] == start:
                plan[-1] = last[:4] + (last[4] + unit,)
            else:
                plan.append((source, start, target, at * unit, unit))
    shapes = tuple(
        jax.ShapeDtypeStruct((len(keys) * unit,) + arrays[0].shape[1:], arrays[0].dtype) for keys in wanted
    )
    any_space = pl.BlockSpec(memory_space=pl.ANY)
    out = pl.pallas_call(
        functools.partial(pack_kernel, plan, len(arrays)),
        out_shape=shapes,
        in_specs=[any_space] * len(arrays),
        out_specs=(any_space,) * len(shapes),
        scratch_shapes=[
            pltpu.VMEM((sum(shape.shape[0] for shape in shapes),) + arrays[0].shape[1:], arrays[0].dtype),
            pltpu.SemaphoreType.DMA((len(plan),)),
            pltpu.SemaphoreType.DMA((len(plan),)),
        ],
        compiler_params=pltpu.CompilerParams(vmem_limit_bytes=SMALL_LIMIT),
        cost_estimate=cost,
        name="pack",
    )(*arrays)
    return [(array, list(keys)) for array, keys in zip(out, wanted, strict=True)]


def segs(dy, dz, quarters):
    return [(dy % SIDE, dz % SIDE, 0, q) for q in quarters]


FIRST, SECOND = (0, 1), (2, 3)
SENDS = [
    [("y", 1, segs(0, 0, range(4))), ("y", -1, segs(0, 0, range(4))), ("z", 1, segs(0, 0, range(4))), ("z", -1, segs(0, 0, range(4)))],
    [
        ("z", 1, segs(1, 0, FIRST) + segs(-1, 0, FIRST) + segs(0, -1, FIRST)),
        ("z", -1, segs(1, 0, FIRST) + segs(-1, 0, FIRST) + segs(0, 1, SECOND)),
        ("y", 1, segs(0, 1, SECOND) + segs(0, -1, SECOND) + segs(-1, 0, FIRST)),
        ("y", -1, segs(0, 1, SECOND) + segs(0, -1, SECOND) + segs(1, 0, SECOND)),
    ],
    [
        ("z", 1, segs(2, 0, FIRST) + segs(1, -1, (0,)) + segs(-1, -1, (0,))),
        ("z", -1, segs(2, 0, FIRST) + segs(1, 1, (1,)) + segs(-1, 1, (1,))),
        ("y", 1, segs(0, 2, SECOND) + segs(-1, 1, (2,)) + segs(-1, -1, (2,))),
        ("y", -1, segs(0, 2, SECOND) + segs(1, 1, (3,)) + segs(1, -1, (3,))),
    ],
    [("z", 1, segs(2, -1, (0,))), ("z", -1, segs(2, 1, (1,))), ("y", 1, segs(-1, 2, (2,))), ("y", -1, segs(1, 2, (3,)))],
]


def ring(own, leaves, turns, beside):
    unit = leaves // QUARTERS
    mine = (own, segs(0, 0, range(QUARTERS)))
    have, others, fresh, done = [mine], [], [mine], []
    payloads = [mine] * len(SENDS[0])
    for number, sends in enumerate(SENDS):
        new = [moved(p, axis, by, lax.ppermute) for p, (axis, by, _) in zip(payloads, sends, strict=True)]
        joined = fresh[0]
        if number > 0:
            joined = packed(fresh, [[key for p in fresh for key in p[1]]], unit)[0]
        swapped = moved(joined, "core", 1, turns)
        done = beside[number](have, others, done)
        wanted = [[key for p in new for key in p[1]]]
        if number + 1 < len(SENDS):
            wanted = [keys for _, _, keys in SENDS[number + 1]]
        following = packed(have + new, wanted, unit, LONG)
        arrays, ahead, other, done = lax.optimization_barrier(
            ([p[0] for p in new], [p[0] for p in following], swapped[0], done)
        )
        fresh = [(array, p[1]) for array, p in zip(arrays, new, strict=True)]
        payloads = [(array, p[1]) for array, p in zip(ahead, following, strict=True)]
        have, others = have + fresh, others + [(other, swapped[1])]
    return have + others + [moved(payloads[0], "core", 1, lax.ppermute)], done


def order_kernel(own_ref, list_ref, mask_ref, pos_ref, code_ref):
    leaves, slots = list_ref.shape
    devices = len(ORDER)
    names = list_ref[...]
    owner = lax.rem(names // leaves, devices)
    code = (lax.rem(names, leaves) * 2 + mask_ref[...]).astype(jnp.float32)
    row = lax.broadcasted_iota(jnp.int32, (leaves, LANES), 0)
    lane = lax.broadcasted_iota(jnp.int32, (leaves, LANES), 1)
    below = (row > lane).astype(jnp.bfloat16)
    own = jnp.broadcast_to(own_ref[...], (leaves, LANES))
    used = jnp.zeros((1, LANES), jnp.float32)
    sorted_codes = jnp.zeros((LANES, LANES), jnp.float32)
    places = jnp.zeros((leaves, LANES), jnp.float32)
    for slot in range(slots):
        named = (owner[:, slot : slot + 1] == own).astype(jnp.float32)
        before = jnp.dot(below, named.astype(jnp.bfloat16), preferred_element_type=jnp.float32) + used
        used = used + jnp.sum(named, axis=0, keepdims=True)
        index = jnp.sum(named * before, axis=1, keepdims=True)
        rank = jnp.sum(named * lane.astype(jnp.float32), axis=1, keepdims=True)
        places = jnp.where(lane == slot, rank * CAP + index, places)
        spread = (lane.astype(jnp.float32) == index).astype(jnp.bfloat16)
        sorted_codes = sorted_codes + lax.dot_general(
            (named * code[:, slot : slot + 1]).astype(jnp.bfloat16),
            spread,
            (((0,), (0,)), ((), ())),
            preferred_element_type=jnp.float32,
        )
    pos_ref[...] = places[:, :slots].astype(jnp.int32)
    code_ref[...] = sorted_codes[:devices].astype(jnp.int32)


def slot_order(leaf_list, leaf_mask, own):
    return pl.pallas_call(
        order_kernel,
        out_shape=(
            jax.ShapeDtypeStruct(leaf_list.shape, jnp.int32),
            jax.ShapeDtypeStruct((len(ORDER), LANES), jnp.int32),
        ),
        compiler_params=pltpu.CompilerParams(vmem_limit_bytes=SMALL_LIMIT),
        cost_estimate=BRIEF,
        name="slot_order",
    )(own, leaf_list, leaf_mask)


def parent_coef_kernel(pair_ref, transfer_ref, out_ref):
    left_r = left_lanes(ROWS)
    for parent in range(out_ref.shape[0]):
        blocks = []
        for leaf in range(CHILD):
            pair = parent * CHILD // 2 + leaf // 2
            x = [pair_ref[pair, pl.ds(a4, ROWS, stride=4), :] for a4 in range(4)]
            if leaf % 2 == 0:
                tiles = [jnp.where(left_r, x[n], pltpu.roll(x[n + 1], NV, 1)) for n in (0, 2)]
            else:
                tiles = [jnp.where(left_r, pltpu.roll(x[n], NV, 1), x[n + 1]) for n in (0, 2)]
            blocks.append(jnp.concatenate(tiles, axis=1))
        coef_high, coef_low = split(jnp.concatenate(blocks, axis=0))
        rows = CHILD * ROWS
        high, low = split(transfer_ref[parent * rows : (parent + 1) * rows])
        full = lax.dot_general(
            jnp.concatenate([high, low, high], axis=0),
            jnp.concatenate([coef_high, coef_high, coef_low], axis=0),
            (((0,), (0,)), ((), ())),
            preferred_element_type=jnp.float32,
        )
        even = full[:K, :LANES] + full[2 * K : 3 * K, LANES:]
        odd = full[K : 2 * K, :LANES] + full[3 * K :, LANES:]
        total = even + pltpu.roll(odd, NV, 1)
        for half in (0, 1):
            first = total[half * TILE : half * TILE + ROWS]
            second = total[half * TILE + ROWS : (half + 1) * TILE]
            out_ref[parent, half * ROWS : (half + 1) * ROWS] = jnp.where(left_r, first, pltpu.roll(second, NV, 1))


def parent_coefs(coef_pairs, rows):
    parents = coef_pairs.shape[0] * 2 // CHILD
    return pl.pallas_call(
        parent_coef_kernel,
        out_shape=jax.ShapeDtypeStruct((parents, TILE, LANES), jnp.float32),
        compiler_params=pltpu.CompilerParams(vmem_limit_bytes=SMALL_LIMIT),
        cost_estimate=BRIEF,
        name="parent_coef",
    )(coef_pairs, rows)


def parent_field_kernel(group, list_ref, mask_ref, branch_ref, *refs):
    coef_refs, (coupling_ref, transfer_ref, down_ref, coef_ref) = refs[:BRANCHES], refs[BRANCHES:]
    parents = coef_ref.shape[0] // BRANCHES
    slots = list_ref.shape[1]
    parent = pl.program_id(0)
    left_k, left_r = left_lanes(K), left_lanes(ROWS)

    @pl.when(parent == 0)
    def _():
        for number, ref in enumerate(coef_refs):
            coef_ref[number * parents : (number + 1) * parents] = ref[...]

    parts = []
    for slot in range(slots):
        name = list_ref[parent, slot]
        at = lax.rem(name // group - branch_ref[0] + BRANCHES, BRANCHES) * parents + lax.rem(name, parents)
        both = coef_ref[at]
        live = mask_ref[parent, slot]
        parts += [pick_slot(both[:ROWS], live, left_r), pick_slot(both[ROWS:], live, left_r)]
    both = jnp.dot(
        jnp.concatenate(split(coupling_ref[0]), axis=0),
        jnp.concatenate(parts, axis=0),
        preferred_element_type=jnp.float32,
    )
    summed = both[:K] + both[K:]
    field = summed + pltpu.roll(summed, NV, 1)
    zero = jnp.zeros_like(field)
    left, right = jnp.where(left_k, field, zero), jnp.where(left_k, zero, field)
    spread = jnp.concatenate(
        [
            jnp.concatenate([left, right, zero, zero], axis=0),
            jnp.concatenate([zero, zero, left, right], axis=0),
        ],
        axis=1,
    )
    spread_high, spread_low = split(spread)
    high, low = split(transfer_ref[...])
    full = jnp.dot(
        jnp.concatenate([high, low, high], axis=1),
        jnp.concatenate([spread_high, spread_high, spread_low], axis=0),
        preferred_element_type=jnp.float32,
    )
    for pair in range(CHILD // 2):
        for a4 in range(4):
            lanes = slice(a4 // 2 * LANES, (a4 // 2 + 1) * LANES)
            even = full[2 * pair * ROWS : (2 * pair + 1) * ROWS, lanes]
            odd = full[(2 * pair + 1) * ROWS : (2 * pair + 2) * ROWS, lanes]
            if a4 % 2 == 0:
                odd = pltpu.roll(odd, NV, 1)
            else:
                even = pltpu.roll(even, NV, 1)
            down_ref[pair, pl.ds(a4, ROWS, stride=4), :] = jnp.where(left_r, even, odd)


def downward_pairs(parent_list, parent_mask, branch, group, coef_all, coupling, rows):
    parents, _, width = coupling.shape
    smem = pl.BlockSpec(memory_space=pltpu.SMEM)
    return pl.pallas_call(
        functools.partial(parent_field_kernel, group),
        out_shape=jax.ShapeDtypeStruct((parents * CHILD // 2, K, LANES), jnp.float32),
        grid=(parents,),
        in_specs=[
            smem,
            smem,
            smem,
        ]
        + [pl.BlockSpec(memory_space=pltpu.VMEM)] * BRANCHES
        + [
            pl.BlockSpec((1, K, width), lambda i: (i, 0, 0)),
            pl.BlockSpec((CHILD * ROWS, LANES), lambda i: (i, 0)),
        ],
        out_specs=pl.BlockSpec((CHILD // 2, K, LANES), lambda i: (i, 0, 0)),
        scratch_shapes=[pltpu.VMEM((BRANCHES * parents, TILE, LANES), jnp.float32)],
        compiler_params=pltpu.CompilerParams(vmem_limit_bytes=SMALL_LIMIT),
        cost_estimate=BRIEF,
        name="parent_field",
    )(parent_list, parent_mask, branch, *coef_all, coupling, rows)


def per_device(
    vectors,
    basis,
    transfer,
    leaf_coupling,
    leaf_list,
    leaf_mask,
    parent_coupling,
    parent_list,
    parent_mask,
):
    leaf_count = leaf_list.shape[0]
    parent_count = parent_list.shape[0]
    subtrees = lax.axis_size("subtree")
    branches = lax.axis_size("branch")
    me = lax.axis_index("subtree")
    here = (me // (2 * SIDE), me // 2 % SIDE, me % 2)

    own = jnp.stack([subtree_index(dy, dz, flip, *here) for dy, dz, flip in ORDER]).astype(jnp.int32)
    own = jnp.pad(own, (0, LANES - len(ORDER)), constant_values=-1)[None, :]
    branch = lax.axis_index("branch").astype(jnp.int32)[None]
    rows = transfer.reshape(parent_count * CHILD * ROWS, LANES)
    coef, coef_pairs = leaf_coefs(basis, vectors, 64)
    turns = Turns()

    def pick(number, flips, codes, pieces):
        devices = [key + (flip,) for flip in flips for key in STAGES[number]]
        return picked_slots(devices, codes, pieces, leaf_count // QUARTERS, leaf_count)

    def beside_first(have, others, done):
        parent_coef = parent_coefs(coef_pairs, rows)
        coef_all = [parent_coef]
        order = ()
        for by in range(1, branches):
            perm = [(i, (i - by) % branches) for i in range(branches)]
            coef_all.append(turns(parent_coef, "branch", perm, order))
            if by == 1:
                order = slot_order(leaf_list, leaf_mask, own)
        return order, coef_all

    def beside_second(have, others, done):
        order, coef_all = done
        down = downward_pairs(
            parent_list, parent_mask, branch, parent_count * subtrees, coef_all, parent_coupling, rows
        )
        return order, down, [pick(0, (0,), order[1], have)]

    def beside_third(have, others, done):
        order, down, tiles = done
        far = pick(0, (1,), order[1], others)
        return order, down, tiles + [far, pick(1, (0,), order[1], have)]

    def beside_fourth(have, others, done):
        order, down, tiles = done
        return order, down, tiles + [pick(1, (1,), order[1], others)]

    pieces, ((pos, codes), down, tiles) = ring(
        coef, leaf_count, turns, [beside_first, beside_second, beside_third, beside_fourth]
    )
    late = ORDER[2 * (len(STAGES[0]) + len(STAGES[1])) :]
    return products(pos, codes, tiles, late, pieces, leaf_coupling, down, basis, 16)


def solution(mesh):
    return jax.shard_map(
        per_device,
        mesh=mesh,
        in_specs=(
            P(None, ("branch", "subtree")),
            P(None, ("branch", "subtree")),
            P(("branch", "subtree"), None),
            P(("branch", "subtree"), None, None),
            P(("branch", "subtree"), None),
            P(("branch", "subtree"), None),
            P(("branch", "subtree"), None, None),
            P(("branch", "subtree"), None),
            P(("branch", "subtree"), None),
        ),
        out_specs=P(None, ("branch", "subtree")),
        check_vma=False,
    )
```

```python
import functools

import jax
import jax.numpy as jnp
from jax import lax
from jax.experimental import pallas as pl
from jax.experimental.pallas import tpu as pltpu
from jax.sharding import PartitionSpec as P

PTS = 64
K = 32
NV = 64
CHILD = 8
ROWS = 8
TILE = 16
LANES = 2 * NV
CAP = 64
SIDE = 4
QUARTERS = 4
BRANCHES = 4

BRIEF = pl.CostEstimate(flops=0, bytes_accessed=0, transcendentals=0)
FINAL_LIMIT = 36 * 2**20
SMALL_LIMIT = 12 * 2**20
WHOLE_LIMIT = 60 * 2**20
LONG = pl.CostEstimate(flops=10**11, bytes_accessed=10**9, transcendentals=0)

CROSS = [(0, 0)]
STEP1 = [(1, 0), (3, 0), (0, 1), (0, 3)]
STEP2 = [(1, 1), (1, 3), (3, 1), (3, 3), (2, 0), (0, 2)]
STEP3 = [(2, 1), (2, 3), (1, 2), (3, 2)]
STEP4 = [(2, 2)]
STAGES = [CROSS + STEP1, STEP2, STEP3, STEP4]
ORDER = [(dy, dz, flip) for stage in STAGES for flip in (0, 1) for dy, dz in stage]


def split(x):
    high = x.astype(jnp.bfloat16)
    low = (x - high.astype(jnp.float32)).astype(jnp.bfloat16)
    return high, low


def left_lanes(rows):
    return lax.broadcasted_iota(jnp.int32, (rows, LANES), 1) < NV


def coef_kernel(basis_ref, vectors_ref, coef_ref, pair_ref):
    left_k = left_lanes(K)
    left_r = left_lanes(ROWS)
    for pair in range(basis_ref.shape[1] // LANES):
        lanes = slice(pair * LANES, (pair + 1) * LANES)
        rows = []
        for part in split(basis_ref[:, lanes]):
            zero = jnp.zeros_like(part)
            rows += [jnp.where(left_k, part, zero), jnp.where(left_k, zero, part)]
        both = lax.dot_general(
            jnp.concatenate(rows, axis=0),
            jnp.concatenate(split(vectors_ref[:, lanes]), axis=0),
            (((1,), (1,)), ((), ())),
            preferred_element_type=jnp.float32,
        )
        even, odd = both[:K] + both[2 * K : 3 * K], both[K : 2 * K] + both[3 * K :]
        even, odd = even + pltpu.roll(even, NV, 1), odd + pltpu.roll(odd, NV, 1)
        pair_ref[pair] = jnp.where(left_k, even, odd)
        for half in (0, 1):
            first = slice(half * TILE, half * TILE + ROWS)
            second = slice(half * TILE + ROWS, (half + 1) * TILE)
            rows = slice(half * ROWS, (half + 1) * ROWS)
            coef_ref[2 * pair, rows] = jnp.where(left_r, even[first], even[second])
            coef_ref[2 * pair + 1, rows] = jnp.where(left_r, odd[first], odd[second])


def leaf_coefs(basis, vectors, block):
    leaves = basis.shape[1] // PTS
    return pl.pallas_call(
        coef_kernel,
        out_shape=(
            jax.ShapeDtypeStruct((leaves, TILE, LANES), jnp.float32),
            jax.ShapeDtypeStruct((leaves // 2, K, LANES), jnp.float32),
        ),
        grid=(leaves // block,),
        in_specs=[
            pl.BlockSpec((K, block * PTS), lambda i: (0, i)),
            pl.BlockSpec((NV, block * PTS), lambda i: (0, i)),
        ],
        out_specs=(
            pl.BlockSpec((block, TILE, LANES), lambda i: (i, 0, 0)),
            pl.BlockSpec((block // 2, K, LANES), lambda i: (i, 0, 0)),
        ),
        compiler_params=pltpu.CompilerParams(vmem_limit_bytes=WHOLE_LIMIT),
        name="leaf_coef",
    )(basis, vectors)


def pick_slot(x, live, left_r):
    x = x * live.astype(jnp.float32)
    high = x.astype(jnp.bfloat16).astype(jnp.float32)
    low = pltpu.roll(x - high, NV, 1)
    return jnp.concatenate([jnp.where(left_r, high, low), jnp.where(left_r, low, high)], axis=0).astype(jnp.bfloat16)


def pick_kernel(plan, first, code_ref, *refs):
    sources, out_ref, held, sem = refs[:-3], refs[-3], refs[-2], refs[-1]
    step = pl.program_id(0)
    left_r = left_lanes(ROWS)

    @pl.when(step == 0)
    def _():
        for device, source, start, target, count in plan:
            pltpu.make_async_copy(
                sources[source].at[pl.ds(start, count)],
                held.at[device, pl.ds(target, count)],
                sem.at[device],
            ).start()

    pltpu.make_async_copy(held.at[step], held.at[step], sem.at[step]).wait()

    @pl.loop(0, CAP // 32)
    def _(part):
        for n in range(32):
            slot = part * 32 + n
            code = code_ref[first + step, slot]
            both = held[step, code >> 1]
            out_ref[slot, :TILE] = pick_slot(both[:ROWS], code & 1, left_r)
            out_ref[slot, TILE:] = pick_slot(both[ROWS:], code & 1, left_r)


def picked_slots(devices, codes, pieces, unit, leaves):
    first = ORDER.index(devices[0])
    arrays, plan = [], []
    for device, key in enumerate(devices):
        for quarter in range(QUARTERS):
            piece, at = next((p, p[1].index(key + (quarter,))) for p in pieces if key + (quarter,) in p[1])
            index = next((i for i, a in enumerate(arrays) if a is piece[0]), None)
            if index is None:
                index = len(arrays)
                arrays.append(piece[0])
            last = plan[-1] if plan else None
            if last and last[0] == device and last[1] == index and last[2] + last[4] == at * unit:
                plan[-1] = last[:4] + (last[4] + unit,)
            else:
                plan.append((device, index, at * unit, quarter * unit, unit))
    count = len(devices)
    return pl.pallas_call(
        functools.partial(pick_kernel, plan, first),
        out_shape=jax.ShapeDtypeStruct((count * CAP, K, LANES), jnp.bfloat16),
        grid=(count,),
        in_specs=[pl.BlockSpec(memory_space=pltpu.SMEM)] + [pl.BlockSpec(memory_space=pl.ANY)] * len(arrays),
        out_specs=pl.BlockSpec((CAP, K, LANES), lambda i: (i, 0, 0)),
        scratch_shapes=[
            pltpu.VMEM((count, leaves, TILE, LANES), jnp.float32),
            pltpu.SemaphoreType.DMA((count,)),
        ],
        compiler_params=pltpu.CompilerParams(vmem_limit_bytes=SMALL_LIMIT),
        cost_estimate=BRIEF,
        name="pick",
    )(codes, *arrays)


def arrival_plan(devices, pieces, unit):
    arrays, plan = [], []
    for rank, key in enumerate(devices):
        for quarter in range(QUARTERS):
            piece, at = next((p, p[1].index(key + (quarter,))) for p in pieces if key + (quarter,) in p[1])
            index = next((i for i, a in enumerate(arrays) if a is piece[0]), None)
            if index is None:
                index = len(arrays)
                arrays.append(piece[0])
            last = plan[-1] if plan else None
            if last and last[:2] == (rank, index) and last[2] + last[4] == at * unit:
                plan[-1] = last[:4] + (last[4] + unit,)
            else:
                plan.append((rank, index, at * unit, quarter * unit, unit))
    return arrays, plan


def field_kernel(slots, block, plan, ready, count, pos_ref, code_ref, *refs):
    pieces, sources = refs[:ready], refs[ready : ready + count]
    coupling_ref, down_ref, basis_ref, out_ref, tiles, held, totals, sem, held_sem = refs[ready + count :]
    step = pl.program_id(0)
    first = step * block
    left_k, left_r, left_v = left_lanes(K), left_lanes(ROWS), left_lanes(NV)

    @pl.when(step == 0)
    def _():
        for device, source, start, target, size in plan:
            pltpu.make_async_copy(
                sources[source].at[pl.ds(start, size)], held.at[device, pl.ds(target, size)], held_sem.at[device]
            ).start()
        copies, at = [], 0
        for piece in pieces:
            copies.append(pltpu.make_async_copy(piece, tiles.at[pl.ds(at, piece.shape[0])], sem.at[len(copies)]))
            at += piece.shape[0]
        for copy in copies:
            copy.start()
        early = at // CAP

        @pl.loop(0, held.shape[0])
        def _(device):
            pltpu.make_async_copy(held.at[device], held.at[device], held_sem.at[device]).wait()
            for slot in range(CAP):
                code = code_ref[early + device, slot]
                both = held[device, code >> 1]
                place = (early + device) * CAP + slot
                tiles[place, :TILE] = pick_slot(both[:ROWS], code & 1, left_r)
                tiles[place, TILE:] = pick_slot(both[ROWS:], code & 1, left_r)

        for copy in copies:
            copy.wait()

    def leaf_field(leaf):
        parts = [tiles[pos_ref[first + leaf, slot]] for slot in range(slots)]
        both = jnp.dot(
            jnp.concatenate(split(coupling_ref[leaf]), axis=0),
            jnp.concatenate(parts, axis=0),
            preferred_element_type=jnp.float32,
        )
        summed = both[:K] + both[K:]
        return summed + pltpu.roll(summed, NV, 1)

    def pair_total(pair):
        return jnp.where(left_k, leaf_field(2 * pair), leaf_field(2 * pair + 1)) + down_ref[pair]

    def diagonal(x):
        rows = []
        for g in range(4):
            row = [x[:, n * LANES : (n + 1) * LANES] if n == g else jnp.zeros((K, LANES), x.dtype) for n in range(4)]
            rows.append(jnp.concatenate(row, axis=1))
        return jnp.concatenate(rows, axis=0)

    def product(quad, total):
        high, low = split(total.T)
        at = pl.multiple_of(quad * 4 * LANES, 4 * LANES)
        basis_high, basis_low = split(basis_ref[:, pl.ds(at, 4 * LANES)])
        spread = diagonal(basis_high)
        both = jnp.dot(
            jnp.concatenate([high, low], axis=1),
            jnp.concatenate([spread, spread], axis=0),
            preferred_element_type=jnp.float32,
        )
        both += jnp.dot(high, diagonal(basis_low), preferred_element_type=jnp.float32)
        for n in range(4):
            square = both[:, n * LANES : (n + 1) * LANES]
            out_ref[:, pl.ds(pl.multiple_of(at + n * LANES, LANES), LANES)] = jnp.where(
                left_v, square[:NV], square[NV:]
            )

    quads = block // 8
    totals_first = step * quads

    @pl.when(step == 0)
    def _():
        totals[...] = jnp.zeros_like(totals)

    @pl.loop(0, quads // 2)
    def _(turn):
        for n in (0, 1):
            quad = totals_first + 2 * turn + n
            before = totals[1 - n]
            for pair in range(4):
                totals[n, pair * K : (pair + 1) * K] = pair_total(8 * turn + 4 * n + pair)
            product(jnp.maximum(quad - 1, 0), before)

    @pl.when(step == pl.num_programs(0) - 1)
    def _():
        product(totals_first + quads - 1, totals[1])


def products(pos, codes, tiles, late, pieces, coupling, down, basis, block):
    leaves, _, width = coupling.shape
    slots = width // K
    arrays, plan = arrival_plan(late, pieces, leaves // QUARTERS)
    smem, hbm = pl.BlockSpec(memory_space=pltpu.SMEM), pl.BlockSpec(memory_space=pl.ANY)
    return pl.pallas_call(
        functools.partial(field_kernel, slots, block, plan, len(tiles), len(arrays)),
        out_shape=jax.ShapeDtypeStruct((NV, leaves * PTS), jnp.float32),
        grid=(leaves // block,),
        in_specs=[smem, smem]
        + [hbm] * (len(tiles) + len(arrays))
        + [
            pl.BlockSpec((block, K, width), lambda i: (i, 0, 0)),
            pl.BlockSpec((block // 2, K, LANES), lambda i: (i, 0, 0)),
            pl.BlockSpec((K, leaves * PTS), lambda i: (0, 0)),
        ],
        out_specs=pl.BlockSpec((NV, leaves * PTS), lambda i: (0, 0)),
        scratch_shapes=[
            pltpu.VMEM((leaves * slots, K, LANES), jnp.bfloat16),
            pltpu.VMEM((len(late), leaves, TILE, LANES), jnp.float32),
            pltpu.VMEM((2, 4 * K, LANES), jnp.float32),
            pltpu.SemaphoreType.DMA((len(tiles),)),
            pltpu.SemaphoreType.DMA((len(late),)),
        ],
        compiler_params=pltpu.CompilerParams(vmem_limit_bytes=FINAL_LIMIT),
        cost_estimate=BRIEF,
        name="leaf_field_product",
    )(pos, codes, *tiles, *arrays, coupling, down, basis)


def subtree_index(dy, dz, flip, z, y, core):
    return (z + dz) % SIDE * (2 * SIDE) + (y + dy) % SIDE * 2 + (core + flip) % 2


def moved(piece, axis, by, send):
    array, segs = piece
    perm, out = [], []
    for z in range(SIDE):
        for y in range(SIDE):
            for core in range(2):
                step = {"y": (by, 0, 0), "z": (0, by, 0), "core": (0, 0, 1)}[axis]
                perm.append((subtree_index(0, 0, 0, z, y, core), subtree_index(*step, z, y, core)))
    for dy, dz, flip, quarter in segs:
        if axis == "y":
            out.append(((dy - by) % SIDE, dz, flip, quarter))
        elif axis == "z":
            out.append((dy, (dz - by) % SIDE, flip, quarter))
        else:
            out.append((dy, dz, 1 - flip, quarter))
    return send(array, "subtree", perm), out


class Turns:
    def __init__(self):
        self.last = None

    def __call__(self, array, axis, perm, after=()):
        if self.last is not None:
            array, _ = lax.optimization_barrier((array, (self.last, after)))
        self.last = lax.ppermute(array, axis, perm)
        return self.last


def pack_kernel(plan, count, *refs):
    sources, targets, (held, read_sem, write_sem) = refs[:count], refs[count:-3], refs[-3:]
    reads, writes, base = [], [], 0
    for number, (source, start, target, at, size) in enumerate(plan):
        place = held.at[pl.ds(base, size)]
        reads.append(pltpu.make_async_copy(sources[source].at[pl.ds(start, size)], place, read_sem.at[number]))
        writes.append(pltpu.make_async_copy(place, targets[target].at[pl.ds(at, size)], write_sem.at[number]))
        base += size
    for read in reads:
        read.start()
    for read, write in zip(reads, writes, strict=True):
        read.wait()
        write.start()
    for write in writes:
        write.wait()


def packed(pieces, wanted, unit, cost=BRIEF):
    arrays, plan = [], []
    for target, keys in enumerate(wanted):
        for at, key in enumerate(keys):
            piece = next(p for p in pieces if key in p[1])
            source = next((i for i, a in enumerate(arrays) if a is piece[0]), None)
            if source is None:
                source = len(arrays)
                arrays.append(piece[0])
            start = piece[1].index(key) * unit
            last = plan[-1] if plan else None
            if last and last[0] == source and last[2] == target and last[1] + last[4] == start:
                plan[-1] = last[:4] + (last[4] + unit,)
            else:
                plan.append((source, start, target, at * unit, unit))
    shapes = tuple(
        jax.ShapeDtypeStruct((len(keys) * unit,) + arrays[0].shape[1:], arrays[0].dtype) for keys in wanted
    )
    any_space = pl.BlockSpec(memory_space=pl.ANY)
    out = pl.pallas_call(
        functools.partial(pack_kernel, plan, len(arrays)),
        out_shape=shapes,
        in_specs=[any_space] * len(arrays),
        out_specs=(any_space,) * len(shapes),
        scratch_shapes=[
            pltpu.VMEM((sum(shape.shape[0] for shape in shapes),) + arrays[0].shape[1:], arrays[0].dtype),
            pltpu.SemaphoreType.DMA((len(plan),)),
            pltpu.SemaphoreType.DMA((len(plan),)),
        ],
        compiler_params=pltpu.CompilerParams(vmem_limit_bytes=SMALL_LIMIT),
        cost_estimate=cost,
        name="pack",
    )(*arrays)
    return [(array, list(keys)) for array, keys in zip(out, wanted, strict=True)]


def segs(dy, dz, quarters):
    return [(dy % SIDE, dz % SIDE, 0, q) for q in quarters]


FIRST, SECOND = (0, 1), (2, 3)
SENDS = [
    [("y", 1, segs(0, 0, range(4))), ("y", -1, segs(0, 0, range(4))), ("z", 1, segs(0, 0, range(4))), ("z", -1, segs(0, 0, range(4)))],
    [
        ("z", 1, segs(1, 0, FIRST) + segs(-1, 0, FIRST) + segs(0, -1, FIRST)),
        ("z", -1, segs(1, 0, FIRST) + segs(-1, 0, FIRST) + segs(0, 1, SECOND)),
        ("y", 1, segs(0, 1, SECOND) + segs(0, -1, SECOND) + segs(-1, 0, FIRST)),
        ("y", -1, segs(0, 1, SECOND) + segs(0, -1, SECOND) + segs(1, 0, SECOND)),
    ],
    [
        ("z", 1, segs(2, 0, FIRST) + segs(1, -1, (0,)) + segs(-1, -1, (0,))),
        ("z", -1, segs(2, 0, FIRST) + segs(1, 1, (1,)) + segs(-1, 1, (1,))),
        ("y", 1, segs(0, 2, SECOND) + segs(-1, 1, (2,)) + segs(-1, -1, (2,))),
        ("y", -1, segs(0, 2, SECOND) + segs(1, 1, (3,)) + segs(1, -1, (3,))),
    ],
    [("z", 1, segs(2, -1, (0,))), ("z", -1, segs(2, 1, (1,))), ("y", 1, segs(-1, 2, (2,))), ("y", -1, segs(1, 2, (3,)))],
]


def ring(own, leaves, turns, beside):
    unit = leaves // QUARTERS
    mine = (own, segs(0, 0, range(QUARTERS)))
    have, others, fresh, done = [mine], [], [mine], []
    payloads = [mine] * len(SENDS[0])
    for number, sends in enumerate(SENDS):
        new = [moved(p, axis, by, lax.ppermute) for p, (axis, by, _) in zip(payloads, sends, strict=True)]
        joined = fresh[0]
        if number > 0:
            joined = packed(fresh, [[key for p in fresh for key in p[1]]], unit)[0]
        swapped = moved(joined, "core", 1, turns)
        done = beside[number](have, others, done)
        wanted = [[key for p in new for key in p[1]]]
        if number + 1 < len(SENDS):
            wanted = [keys for _, _, keys in SENDS[number + 1]]
        following = packed(have + new, wanted, unit, LONG)
        arrays, ahead, other, done = lax.optimization_barrier(
            ([p[0] for p in new], [p[0] for p in following], swapped[0], done)
        )
        fresh = [(array, p[1]) for array, p in zip(arrays, new, strict=True)]
        payloads = [(array, p[1]) for array, p in zip(ahead, following, strict=True)]
        have, others = have + fresh, others + [(other, swapped[1])]
    return have + others + [moved(payloads[0], "core", 1, lax.ppermute)], done


def order_kernel(own_ref, list_ref, mask_ref, pos_ref, code_ref):
    leaves, slots = list_ref.shape
    devices = len(ORDER)
    names = list_ref[...]
    owner = lax.rem(names // leaves, devices)
    code = (lax.rem(names, leaves) * 2 + mask_ref[...]).astype(jnp.float32)
    row = lax.broadcasted_iota(jnp.int32, (leaves, LANES), 0)
    lane = lax.broadcasted_iota(jnp.int32, (leaves, LANES), 1)
    below = (row > lane).astype(jnp.bfloat16)
    own = jnp.broadcast_to(own_ref[...], (leaves, LANES))
    used = jnp.zeros((1, LANES), jnp.float32)
    sorted_codes = jnp.zeros((LANES, LANES), jnp.float32)
    places = jnp.zeros((leaves, LANES), jnp.float32)
    for slot in range(slots):
        named = (owner[:, slot : slot + 1] == own).astype(jnp.float32)
        before = jnp.dot(below, named.astype(jnp.bfloat16), preferred_element_type=jnp.float32) + used
        used = used + jnp.sum(named, axis=0, keepdims=True)
        index = jnp.sum(named * before, axis=1, keepdims=True)
        rank = jnp.sum(named * lane.astype(jnp.float32), axis=1, keepdims=True)
        places = jnp.where(lane == slot, rank * CAP + index, places)
        spread = (lane.astype(jnp.float32) == index).astype(jnp.bfloat16)
        sorted_codes = sorted_codes + lax.dot_general(
            (named * code[:, slot : slot + 1]).astype(jnp.bfloat16),
            spread,
            (((0,), (0,)), ((), ())),
            preferred_element_type=jnp.float32,
        )
    pos_ref[...] = places[:, :slots].astype(jnp.int32)
    code_ref[...] = sorted_codes[:devices].astype(jnp.int32)


def slot_order(leaf_list, leaf_mask, own):
    return pl.pallas_call(
        order_kernel,
        out_shape=(
            jax.ShapeDtypeStruct(leaf_list.shape, jnp.int32),
            jax.ShapeDtypeStruct((len(ORDER), LANES), jnp.int32),
        ),
        compiler_params=pltpu.CompilerParams(vmem_limit_bytes=SMALL_LIMIT),
        cost_estimate=BRIEF,
        name="slot_order",
    )(own, leaf_list, leaf_mask)


def parent_coef_kernel(pair_ref, transfer_ref, out_ref):
    left_r = left_lanes(ROWS)
    for parent in range(out_ref.shape[0]):
        blocks = []
        for leaf in range(CHILD):
            pair = parent * CHILD // 2 + leaf // 2
            x = [pair_ref[pair, pl.ds(a4, ROWS, stride=4), :] for a4 in range(4)]
            if leaf % 2 == 0:
                tiles = [jnp.where(left_r, x[n], pltpu.roll(x[n + 1], NV, 1)) for n in (0, 2)]
            else:
                tiles = [jnp.where(left_r, pltpu.roll(x[n], NV, 1), x[n + 1]) for n in (0, 2)]
            blocks.append(jnp.concatenate(tiles, axis=1))
        coef_high, coef_low = split(jnp.concatenate(blocks, axis=0))
        rows = CHILD * ROWS
        high, low = split(transfer_ref[parent * rows : (parent + 1) * rows])
        full = lax.dot_general(
            jnp.concatenate([high, low, high], axis=0),
            jnp.concatenate([coef_high, coef_high, coef_low], axis=0),
            (((0,), (0,)), ((), ())),
            preferred_element_type=jnp.float32,
        )
        even = full[:K, :LANES] + full[2 * K : 3 * K, LANES:]
        odd = full[K : 2 * K, :LANES] + full[3 * K :, LANES:]
        total = even + pltpu.roll(odd, NV, 1)
        for half in (0, 1):
            first = total[half * TILE : half * TILE + ROWS]
            second = total[half * TILE + ROWS : (half + 1) * TILE]
            out_ref[parent, half * ROWS : (half + 1) * ROWS] = jnp.where(left_r, first, pltpu.roll(second, NV, 1))


def parent_coefs(coef_pairs, rows):
    parents = coef_pairs.shape[0] * 2 // CHILD
    return pl.pallas_call(
        parent_coef_kernel,
        out_shape=jax.ShapeDtypeStruct((parents, TILE, LANES), jnp.float32),
        compiler_params=pltpu.CompilerParams(vmem_limit_bytes=SMALL_LIMIT),
        cost_estimate=BRIEF,
        name="parent_coef",
    )(coef_pairs, rows)


def parent_field_kernel(group, list_ref, mask_ref, branch_ref, *refs):
    coef_refs, (coupling_ref, transfer_ref, down_ref, coef_ref) = refs[:BRANCHES], refs[BRANCHES:]
    parents = coef_ref.shape[0] // BRANCHES
    slots = list_ref.shape[1]
    parent = pl.program_id(0)
    left_k, left_r = left_lanes(K), left_lanes(ROWS)

    @pl.when(parent == 0)
    def _():
        for number, ref in enumerate(coef_refs):
            coef_ref[number * parents : (number + 1) * parents] = ref[...]

    parts = []
    for slot in range(slots):
        name = list_ref[parent, slot]
        at = lax.rem(name // group - branch_ref[0] + BRANCHES, BRANCHES) * parents + lax.rem(name, parents)
        both = coef_ref[at]
        live = mask_ref[parent, slot]
        parts += [pick_slot(both[:ROWS], live, left_r), pick_slot(both[ROWS:], live, left_r)]
    both = jnp.dot(
        jnp.concatenate(split(coupling_ref[0]), axis=0),
        jnp.concatenate(parts, axis=0),
        preferred_element_type=jnp.float32,
    )
    summed = both[:K] + both[K:]
    field = summed + pltpu.roll(summed, NV, 1)
    zero = jnp.zeros_like(field)
    left, right = jnp.where(left_k, field, zero), jnp.where(left_k, zero, field)
    spread = jnp.concatenate(
        [
            jnp.concatenate([left, right, zero, zero], axis=0),
            jnp.concatenate([zero, zero, left, right], axis=0),
        ],
        axis=1,
    )
    spread_high, spread_low = split(spread)
    high, low = split(transfer_ref[...])
    full = jnp.dot(
        jnp.concatenate([high, low, high], axis=1),
        jnp.concatenate([spread_high, spread_high, spread_low], axis=0),
        preferred_element_type=jnp.float32,
    )
    for pair in range(CHILD // 2):
        for a4 in range(4):
            lanes = slice(a4 // 2 * LANES, (a4 // 2 + 1) * LANES)
            even = full[2 * pair * ROWS : (2 * pair + 1) * ROWS, lanes]
            odd = full[(2 * pair + 1) * ROWS : (2 * pair + 2) * ROWS, lanes]
            if a4 % 2 == 0:
                odd = pltpu.roll(odd, NV, 1)
            else:
                even = pltpu.roll(even, NV, 1)
            down_ref[pair, pl.ds(a4, ROWS, stride=4), :] = jnp.where(left_r, even, odd)


def downward_pairs(parent_list, parent_mask, branch, group, coef_all, coupling, rows):
    parents, _, width = coupling.shape
    smem = pl.BlockSpec(memory_space=pltpu.SMEM)
    return pl.pallas_call(
        functools.partial(parent_field_kernel, group),
        out_shape=jax.ShapeDtypeStruct((parents * CHILD // 2, K, LANES), jnp.float32),
        grid=(parents,),
        in_specs=[
            smem,
            smem,
            smem,
        ]
        + [pl.BlockSpec(memory_space=pltpu.VMEM)] * BRANCHES
        + [
            pl.BlockSpec((1, K, width), lambda i: (i, 0, 0)),
            pl.BlockSpec((CHILD * ROWS, LANES), lambda i: (i, 0)),
        ],
        out_specs=pl.BlockSpec((CHILD // 2, K, LANES), lambda i: (i, 0, 0)),
        scratch_shapes=[pltpu.VMEM((BRANCHES * parents, TILE, LANES), jnp.float32)],
        compiler_params=pltpu.CompilerParams(vmem_limit_bytes=SMALL_LIMIT),
        cost_estimate=BRIEF,
        name="parent_field",
    )(parent_list, parent_mask, branch, *coef_all, coupling, rows)


def per_device(
    vectors,
    basis,
    transfer,
    leaf_coupling,
    leaf_list,
    leaf_mask,
    parent_coupling,
    parent_list,
    parent_mask,
):
    leaf_count = leaf_list.shape[0]
    parent_count = parent_list.shape[0]
    subtrees = lax.axis_size("subtree")
    branches = lax.axis_size("branch")
    me = lax.axis_index("subtree")
    here = (me // (2 * SIDE), me // 2 % SIDE, me % 2)

    own = jnp.stack([subtree_index(dy, dz, flip, *here) for dy, dz, flip in ORDER]).astype(jnp.int32)
    own = jnp.pad(own, (0, LANES - len(ORDER)), constant_values=-1)[None, :]
    branch = lax.axis_index("branch").astype(jnp.int32)[None]
    rows = transfer.reshape(parent_count * CHILD * ROWS, LANES)
    coef, coef_pairs = leaf_coefs(basis, vectors, 64)
    turns = Turns()

    def pick(number, flips, codes, pieces):
        devices = [key + (flip,) for flip in flips for key in STAGES[number]]
        return picked_slots(devices, codes, pieces, leaf_count // QUARTERS, leaf_count)

    def beside_first(have, others, done):
        parent_coef = parent_coefs(coef_pairs, rows)
        coef_all = [parent_coef]
        order = ()
        for by in range(1, branches):
            perm = [(i, (i - by) % branches) for i in range(branches)]
            coef_all.append(turns(parent_coef, "branch", perm, order))
            if by == 1:
                order = slot_order(leaf_list, leaf_mask, own)
        return order, coef_all

    def beside_second(have, others, done):
        order, coef_all = done
        down = downward_pairs(
            parent_list, parent_mask, branch, parent_count * subtrees, coef_all, parent_coupling, rows
        )
        return order, down, [pick(0, (0,), order[1], have)]

    def beside_third(have, others, done):
        order, down, tiles = done
        far = pick(0, (1,), order[1], others)
        return order, down, tiles + [far, pick(1, (0,), order[1], have)]

    def beside_fourth(have, others, done):
        order, down, tiles = done
        return order, down, tiles + [pick(1, (1,), order[1], others)]

    pieces, ((pos, codes), down, tiles) = ring(
        coef, leaf_count, turns, [beside_first, beside_second, beside_third, beside_fourth]
    )
    tiles = tiles + [pick(2, (0,), codes, pieces)]
    late = ORDER[2 * (len(STAGES[0]) + len(STAGES[1])) + len(STAGES[2]) :]
    return products(pos, codes, tiles, late, pieces, leaf_coupling, down, basis, 32)


def solution(mesh):
    return jax.shard_map(
        per_device,
        mesh=mesh,
        in_specs=(
            P(None, ("branch", "subtree")),
            P(None, ("branch", "subtree")),
            P(("branch", "subtree"), None),
            P(("branch", "subtree"), None, None),
            P(("branch", "subtree"), None),
            P(("branch", "subtree"), None),
            P(("branch", "subtree"), None, None),
            P(("branch", "subtree"), None),
            P(("branch", "subtree"), None),
        ),
        out_specs=P(None, ("branch", "subtree")),
        check_vma=False,
    )
```

```python
import functools

import jax
import jax.numpy as jnp
from jax import lax
from jax.experimental import pallas as pl
from jax.experimental.pallas import tpu as pltpu
from jax.sharding import PartitionSpec as P

PTS = 64
K = 32
NV = 64
CHILD = 8
ROWS = 8
TILE = 16
LANES = 2 * NV
CAP = 64
SIDE = 4
QUARTERS = 4
BRANCHES = 4

BRIEF = pl.CostEstimate(flops=0, bytes_accessed=0, transcendentals=0)
FINAL_LIMIT = 36 * 2**20
SMALL_LIMIT = 12 * 2**20
WHOLE_LIMIT = 60 * 2**20
LONG = pl.CostEstimate(flops=10**11, bytes_accessed=10**9, transcendentals=0)

CROSS = [(0, 0)]
STEP1 = [(1, 0), (3, 0), (0, 1), (0, 3)]
STEP2 = [(1, 1), (1, 3), (3, 1), (3, 3), (2, 0), (0, 2)]
STEP3 = [(2, 1), (2, 3), (1, 2), (3, 2)]
STEP4 = [(2, 2)]
STAGES = [CROSS + STEP1, STEP2, STEP3, STEP4]
ORDER = [(dy, dz, flip) for stage in STAGES for flip in (0, 1) for dy, dz in stage]


def split(x):
    high = x.astype(jnp.bfloat16)
    low = (x - high.astype(jnp.float32)).astype(jnp.bfloat16)
    return high, low


def left_lanes(rows):
    return lax.broadcasted_iota(jnp.int32, (rows, LANES), 1) < NV


def coef_kernel(basis_ref, vectors_ref, coef_ref, pair_ref):
    left_k = left_lanes(K)
    left_r = left_lanes(ROWS)
    for pair in range(basis_ref.shape[1] // LANES):
        lanes = slice(pair * LANES, (pair + 1) * LANES)
        rows = []
        for part in split(basis_ref[:, lanes]):
            zero = jnp.zeros_like(part)
            rows += [jnp.where(left_k, part, zero), jnp.where(left_k, zero, part)]
        both = lax.dot_general(
            jnp.concatenate(rows, axis=0),
            jnp.concatenate(split(vectors_ref[:, lanes]), axis=0),
            (((1,), (1,)), ((), ())),
            preferred_element_type=jnp.float32,
        )
        even, odd = both[:K] + both[2 * K : 3 * K], both[K : 2 * K] + both[3 * K :]
        even, odd = even + pltpu.roll(even, NV, 1), odd + pltpu.roll(odd, NV, 1)
        pair_ref[pair] = jnp.where(left_k, even, odd)
        for half in (0, 1):
            first = slice(half * TILE, half * TILE + ROWS)
            second = slice(half * TILE + ROWS, (half + 1) * TILE)
            rows = slice(half * ROWS, (half + 1) * ROWS)
            coef_ref[2 * pair, rows] = jnp.where(left_r, even[first], even[second])
            coef_ref[2 * pair + 1, rows] = jnp.where(left_r, odd[first], odd[second])


def leaf_coefs(basis, vectors, block):
    leaves = basis.shape[1] // PTS
    return pl.pallas_call(
        coef_kernel,
        out_shape=(
            jax.ShapeDtypeStruct((leaves, TILE, LANES), jnp.float32),
            jax.ShapeDtypeStruct((leaves // 2, K, LANES), jnp.float32),
        ),
        grid=(leaves // block,),
        in_specs=[
            pl.BlockSpec((K, block * PTS), lambda i: (0, i)),
            pl.BlockSpec((NV, block * PTS), lambda i: (0, i)),
        ],
        out_specs=(
            pl.BlockSpec((block, TILE, LANES), lambda i: (i, 0, 0)),
            pl.BlockSpec((block // 2, K, LANES), lambda i: (i, 0, 0)),
        ),
        compiler_params=pltpu.CompilerParams(vmem_limit_bytes=WHOLE_LIMIT),
        name="leaf_coef",
    )(basis, vectors)


def pick_slot(x, live, left_r):
    x = x * live.astype(jnp.float32)
    high = x.astype(jnp.bfloat16).astype(jnp.float32)
    low = pltpu.roll(x - high, NV, 1)
    return jnp.concatenate([jnp.where(left_r, high, low), jnp.where(left_r, low, high)], axis=0).astype(jnp.bfloat16)


def pick_kernel(plan, first, code_ref, *refs):
    sources, out_ref, held, sem = refs[:-3], refs[-3], refs[-2], refs[-1]
    step = pl.program_id(0)
    left_r = left_lanes(ROWS)

    @pl.when(step == 0)
    def _():
        for device, source, start, target, count in plan:
            pltpu.make_async_copy(
                sources[source].at[pl.ds(start, count)],
                held.at[device, pl.ds(target, count)],
                sem.at[device],
            ).start()

    pltpu.make_async_copy(held.at[step], held.at[step], sem.at[step]).wait()

    @pl.loop(0, CAP // 32)
    def _(part):
        for n in range(32):
            slot = part * 32 + n
            code = code_ref[first + step, slot]
            both = held[step, code >> 1]
            out_ref[slot, :TILE] = pick_slot(both[:ROWS], code & 1, left_r)
            out_ref[slot, TILE:] = pick_slot(both[ROWS:], code & 1, left_r)


def picked_slots(devices, codes, pieces, unit, leaves):
    first = ORDER.index(devices[0])
    arrays, plan = [], []
    for device, key in enumerate(devices):
        for quarter in range(QUARTERS):
            piece, at = next((p, p[1].index(key + (quarter,))) for p in pieces if key + (quarter,) in p[1])
            index = next((i for i, a in enumerate(arrays) if a is piece[0]), None)
            if index is None:
                index = len(arrays)
                arrays.append(piece[0])
            last = plan[-1] if plan else None
            if last and last[0] == device and last[1] == index and last[2] + last[4] == at * unit:
                plan[-1] = last[:4] + (last[4] + unit,)
            else:
                plan.append((device, index, at * unit, quarter * unit, unit))
    count = len(devices)
    return pl.pallas_call(
        functools.partial(pick_kernel, plan, first),
        out_shape=jax.ShapeDtypeStruct((count * CAP, K, LANES), jnp.bfloat16),
        grid=(count,),
        in_specs=[pl.BlockSpec(memory_space=pltpu.SMEM)] + [pl.BlockSpec(memory_space=pl.ANY)] * len(arrays),
        out_specs=pl.BlockSpec((CAP, K, LANES), lambda i: (i, 0, 0)),
        scratch_shapes=[
            pltpu.VMEM((count, leaves, TILE, LANES), jnp.float32),
            pltpu.SemaphoreType.DMA((count,)),
        ],
        compiler_params=pltpu.CompilerParams(vmem_limit_bytes=SMALL_LIMIT),
        cost_estimate=BRIEF,
        name="pick",
    )(codes, *arrays)


def arrival_plan(devices, pieces, unit):
    arrays, plan = [], []
    for rank, key in enumerate(devices):
        for quarter in range(QUARTERS):
            piece, at = next((p, p[1].index(key + (quarter,))) for p in pieces if key + (quarter,) in p[1])
            index = next((i for i, a in enumerate(arrays) if a is piece[0]), None)
            if index is None:
                index = len(arrays)
                arrays.append(piece[0])
            last = plan[-1] if plan else None
            if last and last[:2] == (rank, index) and last[2] + last[4] == at * unit:
                plan[-1] = last[:4] + (last[4] + unit,)
            else:
                plan.append((rank, index, at * unit, quarter * unit, unit))
    return arrays, plan


def field_kernel(slots, block, plan, ready, count, pos_ref, code_ref, *refs):
    pieces, sources = refs[:ready], refs[ready : ready + count]
    coupling_ref, down_ref, basis_ref, out_ref, tiles, held, totals, sem, held_sem = refs[ready + count :]
    step = pl.program_id(0)
    first = step * block
    left_k, left_r, left_v = left_lanes(K), left_lanes(ROWS), left_lanes(NV)

    @pl.when(step == 0)
    def _():
        for device, source, start, target, size in plan:
            pltpu.make_async_copy(
                sources[source].at[pl.ds(start, size)], held.at[device, pl.ds(target, size)], held_sem.at[device]
            ).start()
        copies, at = [], 0
        for piece in pieces:
            copies.append(pltpu.make_async_copy(piece, tiles.at[pl.ds(at, piece.shape[0])], sem.at[len(copies)]))
            at += piece.shape[0]
        for copy in copies:
            copy.start()
        early = at // CAP

        @pl.loop(0, held.shape[0])
        def _(device):
            pltpu.make_async_copy(held.at[device], held.at[device], held_sem.at[device]).wait()
            for slot in range(CAP):
                code = code_ref[early + device, slot]
                both = held[device, code >> 1]
                place = (early + device) * CAP + slot
                tiles[place, :TILE] = pick_slot(both[:ROWS], code & 1, left_r)
                tiles[place, TILE:] = pick_slot(both[ROWS:], code & 1, left_r)

        for copy in copies:
            copy.wait()

    def leaf_field(leaf):
        parts = [tiles[pos_ref[first + leaf, slot]] for slot in range(slots)]
        both = jnp.dot(
            jnp.concatenate(split(coupling_ref[leaf]), axis=0),
            jnp.concatenate(parts, axis=0),
            preferred_element_type=jnp.float32,
        )
        summed = both[:K] + both[K:]
        return summed + pltpu.roll(summed, NV, 1)

    def pair_total(pair):
        return jnp.where(left_k, leaf_field(2 * pair), leaf_field(2 * pair + 1)) + down_ref[pair]

    def diagonal(x):
        rows = []
        for g in range(4):
            row = [x[:, n * LANES : (n + 1) * LANES] if n == g else jnp.zeros((K, LANES), x.dtype) for n in range(4)]
            rows.append(jnp.concatenate(row, axis=1))
        return jnp.concatenate(rows, axis=0)

    def product(quad, total):
        high, low = split(total.T)
        at = pl.multiple_of(quad * 4 * LANES, 4 * LANES)
        basis_high, basis_low = split(basis_ref[:, pl.ds(at, 4 * LANES)])
        spread = diagonal(basis_high)
        both = jnp.dot(
            jnp.concatenate([high, low], axis=1),
            jnp.concatenate([spread, spread], axis=0),
            preferred_element_type=jnp.float32,
        )
        both += jnp.dot(high, diagonal(basis_low), preferred_element_type=jnp.float32)
        for n in range(4):
            square = both[:, n * LANES : (n + 1) * LANES]
            out_ref[:, pl.ds(pl.multiple_of(at + n * LANES, LANES), LANES)] = jnp.where(
                left_v, square[:NV], square[NV:]
            )

    quads = block // 8
    totals_first = step * quads

    @pl.when(step == 0)
    def _():
        totals[...] = jnp.zeros_like(totals)

    @pl.loop(0, quads // 2)
    def _(turn):
        for n in (0, 1):
            quad = totals_first + 2 * turn + n
            before = totals[1 - n]
            for pair in range(4):
                totals[n, pair * K : (pair + 1) * K] = pair_total(8 * turn + 4 * n + pair)
            product(jnp.maximum(quad - 1, 0), before)

    @pl.when(step == pl.num_programs(0) - 1)
    def _():
        product(totals_first + quads - 1, totals[1])


def products(pos, codes, tiles, late, pieces, coupling, down, basis, block):
    leaves, _, width = coupling.shape
    slots = width // K
    arrays, plan = arrival_plan(late, pieces, leaves // QUARTERS)
    smem, hbm = pl.BlockSpec(memory_space=pltpu.SMEM), pl.BlockSpec(memory_space=pl.ANY)
    return pl.pallas_call(
        functools.partial(field_kernel, slots, block, plan, len(tiles), len(arrays)),
        out_shape=jax.ShapeDtypeStruct((NV, leaves * PTS), jnp.float32),
        grid=(leaves // block,),
        in_specs=[smem, smem]
        + [hbm] * (len(tiles) + len(arrays))
        + [
            pl.BlockSpec((block, K, width), lambda i: (i, 0, 0)),
            pl.BlockSpec((block // 2, K, LANES), lambda i: (i, 0, 0)),
            pl.BlockSpec((K, leaves * PTS), lambda i: (0, 0)),
        ],
        out_specs=pl.BlockSpec((NV, leaves * PTS), lambda i: (0, 0)),
        scratch_shapes=[
            pltpu.VMEM((leaves * slots, K, LANES), jnp.bfloat16),
            pltpu.VMEM((len(late), leaves, TILE, LANES), jnp.float32),
            pltpu.VMEM((2, 4 * K, LANES), jnp.float32),
            pltpu.SemaphoreType.DMA((len(tiles),)),
            pltpu.SemaphoreType.DMA((len(late),)),
        ],
        compiler_params=pltpu.CompilerParams(vmem_limit_bytes=FINAL_LIMIT),
        cost_estimate=BRIEF,
        name="leaf_field_product",
    )(pos, codes, *tiles, *arrays, coupling, down, basis)


def subtree_index(dy, dz, flip, z, y, core):
    return (z + dz) % SIDE * (2 * SIDE) + (y + dy) % SIDE * 2 + (core + flip) % 2


def moved(piece, axis, by, send):
    array, segs = piece
    perm, out = [], []
    for z in range(SIDE):
        for y in range(SIDE):
            for core in range(2):
                step = {"y": (by, 0, 0), "z": (0, by, 0), "core": (0, 0, 1)}[axis]
                perm.append((subtree_index(0, 0, 0, z, y, core), subtree_index(*step, z, y, core)))
    for dy, dz, flip, quarter in segs:
        if axis == "y":
            out.append(((dy - by) % SIDE, dz, flip, quarter))
        elif axis == "z":
            out.append((dy, (dz - by) % SIDE, flip, quarter))
        else:
            out.append((dy, dz, 1 - flip, quarter))
    return send(array, "subtree", perm), out


class Turns:
    def __init__(self):
        self.last = None

    def __call__(self, array, axis, perm, after=()):
        if self.last is not None:
            array, _ = lax.optimization_barrier((array, (self.last, after)))
        self.last = lax.ppermute(array, axis, perm)
        return self.last


def pack_kernel(plan, count, *refs):
    sources, targets, (held, read_sem, write_sem) = refs[:count], refs[count:-3], refs[-3:]
    reads, writes, base = [], [], 0
    for number, (source, start, target, at, size) in enumerate(plan):
        place = held.at[pl.ds(base, size)]
        reads.append(pltpu.make_async_copy(sources[source].at[pl.ds(start, size)], place, read_sem.at[number]))
        writes.append(pltpu.make_async_copy(place, targets[target].at[pl.ds(at, size)], write_sem.at[number]))
        base += size
    for read in reads:
        read.start()
    for read, write in zip(reads, writes, strict=True):
        read.wait()
        write.start()
    for write in writes:
        write.wait()


def packed(pieces, wanted, unit, cost=BRIEF):
    arrays, plan = [], []
    for target, keys in enumerate(wanted):
        for at, key in enumerate(keys):
            piece = next(p for p in pieces if key in p[1])
            source = next((i for i, a in enumerate(arrays) if a is piece[0]), None)
            if source is None:
                source = len(arrays)
                arrays.append(piece[0])
            start = piece[1].index(key) * unit
            last = plan[-1] if plan else None
            if last and last[0] == source and last[2] == target and last[1] + last[4] == start:
                plan[-1] = last[:4] + (last[4] + unit,)
            else:
                plan.append((source, start, target, at * unit, unit))
    shapes = tuple(
        jax.ShapeDtypeStruct((len(keys) * unit,) + arrays[0].shape[1:], arrays[0].dtype) for keys in wanted
    )
    any_space = pl.BlockSpec(memory_space=pl.ANY)
    out = pl.pallas_call(
        functools.partial(pack_kernel, plan, len(arrays)),
        out_shape=shapes,
        in_specs=[any_space] * len(arrays),
        out_specs=(any_space,) * len(shapes),
        scratch_shapes=[
            pltpu.VMEM((sum(shape.shape[0] for shape in shapes),) + arrays[0].shape[1:], arrays[0].dtype),
            pltpu.SemaphoreType.DMA((len(plan),)),
            pltpu.SemaphoreType.DMA((len(plan),)),
        ],
        compiler_params=pltpu.CompilerParams(vmem_limit_bytes=SMALL_LIMIT),
        cost_estimate=cost,
        name="pack",
    )(*arrays)
    return [(array, list(keys)) for array, keys in zip(out, wanted, strict=True)]


def segs(dy, dz, quarters):
    return [(dy % SIDE, dz % SIDE, 0, q) for q in quarters]


FIRST, SECOND = (0, 1), (2, 3)
SENDS = [
    [("y", 1, segs(0, 0, range(4))), ("y", -1, segs(0, 0, range(4))), ("z", 1, segs(0, 0, range(4))), ("z", -1, segs(0, 0, range(4)))],
    [
        ("z", 1, segs(1, 0, FIRST) + segs(-1, 0, FIRST) + segs(0, -1, FIRST)),
        ("z", -1, segs(1, 0, FIRST) + segs(-1, 0, FIRST) + segs(0, 1, SECOND)),
        ("y", 1, segs(0, 1, SECOND) + segs(0, -1, SECOND) + segs(-1, 0, FIRST)),
        ("y", -1, segs(0, 1, SECOND) + segs(0, -1, SECOND) + segs(1, 0, SECOND)),
    ],
    [
        ("z", 1, segs(2, 0, FIRST) + segs(1, -1, (0,)) + segs(-1, -1, (0,))),
        ("z", -1, segs(2, 0, FIRST) + segs(1, 1, (1,)) + segs(-1, 1, (1,))),
        ("y", 1, segs(0, 2, SECOND) + segs(-1, 1, (2,)) + segs(-1, -1, (2,))),
        ("y", -1, segs(0, 2, SECOND) + segs(1, 1, (3,)) + segs(1, -1, (3,))),
    ],
    [("z", 1, segs(2, -1, (0,))), ("z", -1, segs(2, 1, (1,))), ("y", 1, segs(-1, 2, (2,))), ("y", -1, segs(1, 2, (3,)))],
]


def ring(own, leaves, turns, beside):
    unit = leaves // QUARTERS
    mine = (own, segs(0, 0, range(QUARTERS)))
    have, others, fresh, done = [mine], [], [mine], []
    payloads = [mine] * len(SENDS[0])
    for number, sends in enumerate(SENDS):
        new = [moved(p, axis, by, lax.ppermute) for p, (axis, by, _) in zip(payloads, sends, strict=True)]
        joined = fresh[0]
        if number > 0:
            joined = packed(fresh, [[key for p in fresh for key in p[1]]], unit)[0]
        swapped = moved(joined, "core", 1, turns)
        done = beside[number](have, others, done)
        if number + 1 < len(SENDS):
            following = packed(have + new, [keys for _, _, keys in SENDS[number + 1]], unit, LONG)
        else:
            following = packed(new, [[key for p in new for key in p[1]]], unit)
        arrays, ahead, other, done = lax.optimization_barrier(
            ([p[0] for p in new], [p[0] for p in following], swapped[0], done)
        )
        fresh = [(array, p[1]) for array, p in zip(arrays, new, strict=True)]
        payloads = [(array, p[1]) for array, p in zip(ahead, following, strict=True)]
        have, others = have + fresh, others + [(other, swapped[1])]
    return have + others + [moved(payloads[0], "core", 1, lax.ppermute)], done


def order_kernel(own_ref, list_ref, mask_ref, pos_ref, code_ref):
    leaves, slots = list_ref.shape
    devices = len(ORDER)
    names = list_ref[...]
    owner = lax.rem(names // leaves, devices)
    code = (lax.rem(names, leaves) * 2 + mask_ref[...]).astype(jnp.float32)
    row = lax.broadcasted_iota(jnp.int32, (leaves, LANES), 0)
    lane = lax.broadcasted_iota(jnp.int32, (leaves, LANES), 1)
    below = (row > lane).astype(jnp.bfloat16)
    own = jnp.broadcast_to(own_ref[...], (leaves, LANES))
    used = jnp.zeros((1, LANES), jnp.float32)
    sorted_codes = jnp.zeros((LANES, LANES), jnp.float32)
    places = jnp.zeros((leaves, LANES), jnp.float32)
    for slot in range(slots):
        named = (owner[:, slot : slot + 1] == own).astype(jnp.float32)
        before = jnp.dot(below, named.astype(jnp.bfloat16), preferred_element_type=jnp.float32) + used
        used = used + jnp.sum(named, axis=0, keepdims=True)
        index = jnp.sum(named * before, axis=1, keepdims=True)
        rank = jnp.sum(named * lane.astype(jnp.float32), axis=1, keepdims=True)
        places = jnp.where(lane == slot, rank * CAP + index, places)
        spread = (lane.astype(jnp.float32) == index).astype(jnp.bfloat16)
        sorted_codes = sorted_codes + lax.dot_general(
            (named * code[:, slot : slot + 1]).astype(jnp.bfloat16),
            spread,
            (((0,), (0,)), ((), ())),
            preferred_element_type=jnp.float32,
        )
    pos_ref[...] = places[:, :slots].astype(jnp.int32)
    code_ref[...] = sorted_codes[:devices].astype(jnp.int32)


def slot_order(leaf_list, leaf_mask, own):
    return pl.pallas_call(
        order_kernel,
        out_shape=(
            jax.ShapeDtypeStruct(leaf_list.shape, jnp.int32),
            jax.ShapeDtypeStruct((len(ORDER), LANES), jnp.int32),
        ),
        compiler_params=pltpu.CompilerParams(vmem_limit_bytes=SMALL_LIMIT),
        cost_estimate=BRIEF,
        name="slot_order",
    )(own, leaf_list, leaf_mask)


def parent_coef_kernel(pair_ref, transfer_ref, out_ref):
    left_r = left_lanes(ROWS)
    for parent in range(out_ref.shape[0]):
        blocks = []
        for leaf in range(CHILD):
            pair = parent * CHILD // 2 + leaf // 2
            x = [pair_ref[pair, pl.ds(a4, ROWS, stride=4), :] for a4 in range(4)]
            if leaf % 2 == 0:
                tiles = [jnp.where(left_r, x[n], pltpu.roll(x[n + 1], NV, 1)) for n in (0, 2)]
            else:
                tiles = [jnp.where(left_r, pltpu.roll(x[n], NV, 1), x[n + 1]) for n in (0, 2)]
            blocks.append(jnp.concatenate(tiles, axis=1))
        coef_high, coef_low = split(jnp.concatenate(blocks, axis=0))
        rows = CHILD * ROWS
        high, low = split(transfer_ref[parent * rows : (parent + 1) * rows])
        full = lax.dot_general(
            jnp.concatenate([high, low, high], axis=0),
            jnp.concatenate([coef_high, coef_high, coef_low], axis=0),
            (((0,), (0,)), ((), ())),
            preferred_element_type=jnp.float32,
        )
        even = full[:K, :LANES] + full[2 * K : 3 * K, LANES:]
        odd = full[K : 2 * K, :LANES] + full[3 * K :, LANES:]
        total = even + pltpu.roll(odd, NV, 1)
        for half in (0, 1):
            first = total[half * TILE : half * TILE + ROWS]
            second = total[half * TILE + ROWS : (half + 1) * TILE]
            out_ref[parent, half * ROWS : (half + 1) * ROWS] = jnp.where(left_r, first, pltpu.roll(second, NV, 1))


def parent_coefs(coef_pairs, rows):
    parents = coef_pairs.shape[0] * 2 // CHILD
    return pl.pallas_call(
        parent_coef_kernel,
        out_shape=jax.ShapeDtypeStruct((parents, TILE, LANES), jnp.float32),
        compiler_params=pltpu.CompilerParams(vmem_limit_bytes=SMALL_LIMIT),
        cost_estimate=BRIEF,
        name="parent_coef",
    )(coef_pairs, rows)


def parent_field_kernel(group, list_ref, mask_ref, branch_ref, *refs):
    coef_refs, (coupling_ref, transfer_ref, down_ref, coef_ref) = refs[:BRANCHES], refs[BRANCHES:]
    parents = coef_ref.shape[0] // BRANCHES
    slots = list_ref.shape[1]
    parent = pl.program_id(0)
    left_k, left_r = left_lanes(K), left_lanes(ROWS)

    @pl.when(parent == 0)
    def _():
        for number, ref in enumerate(coef_refs):
            coef_ref[number * parents : (number + 1) * parents] = ref[...]

    parts = []
    for slot in range(slots):
        name = list_ref[parent, slot]
        at = lax.rem(name // group - branch_ref[0] + BRANCHES, BRANCHES) * parents + lax.rem(name, parents)
        both = coef_ref[at]
        live = mask_ref[parent, slot]
        parts += [pick_slot(both[:ROWS], live, left_r), pick_slot(both[ROWS:], live, left_r)]
    both = jnp.dot(
        jnp.concatenate(split(coupling_ref[0]), axis=0),
        jnp.concatenate(parts, axis=0),
        preferred_element_type=jnp.float32,
    )
    summed = both[:K] + both[K:]
    field = summed + pltpu.roll(summed, NV, 1)
    zero = jnp.zeros_like(field)
    left, right = jnp.where(left_k, field, zero), jnp.where(left_k, zero, field)
    spread = jnp.concatenate(
        [
            jnp.concatenate([left, right, zero, zero], axis=0),
            jnp.concatenate([zero, zero, left, right], axis=0),
        ],
        axis=1,
    )
    spread_high, spread_low = split(spread)
    high, low = split(transfer_ref[...])
    full = jnp.dot(
        jnp.concatenate([high, low, high], axis=1),
        jnp.concatenate([spread_high, spread_high, spread_low], axis=0),
        preferred_element_type=jnp.float32,
    )
    for pair in range(CHILD // 2):
        for a4 in range(4):
            lanes = slice(a4 // 2 * LANES, (a4 // 2 + 1) * LANES)
            even = full[2 * pair * ROWS : (2 * pair + 1) * ROWS, lanes]
            odd = full[(2 * pair + 1) * ROWS : (2 * pair + 2) * ROWS, lanes]
            if a4 % 2 == 0:
                odd = pltpu.roll(odd, NV, 1)
            else:
                even = pltpu.roll(even, NV, 1)
            down_ref[pair, pl.ds(a4, ROWS, stride=4), :] = jnp.where(left_r, even, odd)


def downward_pairs(parent_list, parent_mask, branch, group, coef_all, coupling, rows):
    parents, _, width = coupling.shape
    smem = pl.BlockSpec(memory_space=pltpu.SMEM)
    return pl.pallas_call(
        functools.partial(parent_field_kernel, group),
        out_shape=jax.ShapeDtypeStruct((parents * CHILD // 2, K, LANES), jnp.float32),
        grid=(parents,),
        in_specs=[
            smem,
            smem,
            smem,
        ]
        + [pl.BlockSpec(memory_space=pltpu.VMEM)] * BRANCHES
        + [
            pl.BlockSpec((1, K, width), lambda i: (i, 0, 0)),
            pl.BlockSpec((CHILD * ROWS, LANES), lambda i: (i, 0)),
        ],
        out_specs=pl.BlockSpec((CHILD // 2, K, LANES), lambda i: (i, 0, 0)),
        scratch_shapes=[pltpu.VMEM((BRANCHES * parents, TILE, LANES), jnp.float32)],
        compiler_params=pltpu.CompilerParams(vmem_limit_bytes=SMALL_LIMIT),
        cost_estimate=BRIEF,
        name="parent_field",
    )(parent_list, parent_mask, branch, *coef_all, coupling, rows)


def per_device(
    vectors,
    basis,
    transfer,
    leaf_coupling,
    leaf_list,
    leaf_mask,
    parent_coupling,
    parent_list,
    parent_mask,
):
    leaf_count = leaf_list.shape[0]
    parent_count = parent_list.shape[0]
    subtrees = lax.axis_size("subtree")
    branches = lax.axis_size("branch")
    me = lax.axis_index("subtree")
    here = (me // (2 * SIDE), me // 2 % SIDE, me % 2)

    own = jnp.stack([subtree_index(dy, dz, flip, *here) for dy, dz, flip in ORDER]).astype(jnp.int32)
    own = jnp.pad(own, (0, LANES - len(ORDER)), constant_values=-1)[None, :]
    branch = lax.axis_index("branch").astype(jnp.int32)[None]
    rows = transfer.reshape(parent_count * CHILD * ROWS, LANES)
    coef, coef_pairs = leaf_coefs(basis, vectors, 64)
    turns = Turns()

    def pick(number, flips, codes, pieces):
        devices = [key + (flip,) for flip in flips for key in STAGES[number]]
        return picked_slots(devices, codes, pieces, leaf_count // QUARTERS, leaf_count)

    def beside_first(have, others, done):
        parent_coef = parent_coefs(coef_pairs, rows)
        coef_all = [parent_coef]
        order = ()
        for by in range(1, branches):
            perm = [(i, (i - by) % branches) for i in range(branches)]
            coef_all.append(turns(parent_coef, "branch", perm, order))
            if by == 1:
                order = slot_order(leaf_list, leaf_mask, own)
        return order, coef_all

    def beside_second(have, others, done):
        order, coef_all = done
        down = downward_pairs(
            parent_list, parent_mask, branch, parent_count * subtrees, coef_all, parent_coupling, rows
        )
        return order, down, [pick(0, (0,), order[1], have)]

    def beside_third(have, others, done):
        order, down, tiles = done
        far = pick(0, (1,), order[1], others)
        return order, down, tiles + [far, pick(1, (0,), order[1], have)]

    def beside_fourth(have, others, done):
        order, down, tiles = done
        return order, down, tiles + [pick(1, (1,), order[1], others)]

    pieces, ((pos, codes), down, tiles) = ring(
        coef, leaf_count, turns, [beside_first, beside_second, beside_third, beside_fourth]
    )
    tiles = tiles + [pick(2, (0,), codes, pieces)]
    late = ORDER[2 * (len(STAGES[0]) + len(STAGES[1])) + len(STAGES[2]) :]
    return products(pos, codes, tiles, late, pieces, leaf_coupling, down, basis, 32)


def solution(mesh):
    return jax.shard_map(
        per_device,
        mesh=mesh,
        in_specs=(
            P(None, ("branch", "subtree")),
            P(None, ("branch", "subtree")),
            P(("branch", "subtree"), None),
            P(("branch", "subtree"), None, None),
            P(("branch", "subtree"), None),
            P(("branch", "subtree"), None),
            P(("branch", "subtree"), None, None),
            P(("branch", "subtree"), None),
            P(("branch", "subtree"), None),
        ),
        out_specs=P(None, ("branch", "subtree")),
        check_vma=False,
    )
```

```python
import functools

import jax
import jax.numpy as jnp
from jax import lax
from jax.experimental import pallas as pl
from jax.experimental.pallas import tpu as pltpu
from jax.sharding import PartitionSpec as P

PTS = 64
K = 32
NV = 64
CHILD = 8
ROWS = 8
TILE = 16
LANES = 2 * NV
CAP = 64
SIDE = 4
QUARTERS = 4
BRANCHES = 4

BRIEF = pl.CostEstimate(flops=0, bytes_accessed=0, transcendentals=0)
FINAL_LIMIT = 36 * 2**20
SMALL_LIMIT = 12 * 2**20
WHOLE_LIMIT = 60 * 2**20
LONG = pl.CostEstimate(flops=10**11, bytes_accessed=10**9, transcendentals=0)

CROSS = [(0, 0)]
STEP1 = [(1, 0), (3, 0), (0, 1), (0, 3)]
STEP2 = [(1, 1), (1, 3), (3, 1), (3, 3), (2, 0), (0, 2)]
STEP3 = [(2, 1), (2, 3), (1, 2), (3, 2)]
STEP4 = [(2, 2)]
STAGES = [CROSS + STEP1, STEP2, STEP3, STEP4]
ORDER = [(dy, dz, flip) for stage in STAGES for flip in (0, 1) for dy, dz in stage]


def split(x):
    high = x.astype(jnp.bfloat16)
    low = (x - high.astype(jnp.float32)).astype(jnp.bfloat16)
    return high, low


def left_lanes(rows):
    return lax.broadcasted_iota(jnp.int32, (rows, LANES), 1) < NV


def coef_kernel(basis_ref, vectors_ref, coef_ref, pair_ref):
    left_k = left_lanes(K)
    left_r = left_lanes(ROWS)
    for pair in range(basis_ref.shape[1] // LANES):
        lanes = slice(pair * LANES, (pair + 1) * LANES)
        rows = []
        for part in split(basis_ref[:, lanes]):
            zero = jnp.zeros_like(part)
            rows += [jnp.where(left_k, part, zero), jnp.where(left_k, zero, part)]
        both = lax.dot_general(
            jnp.concatenate(rows, axis=0),
            jnp.concatenate(split(vectors_ref[:, lanes]), axis=0),
            (((1,), (1,)), ((), ())),
            preferred_element_type=jnp.float32,
        )
        even, odd = both[:K] + both[2 * K : 3 * K], both[K : 2 * K] + both[3 * K :]
        even, odd = even + pltpu.roll(even, NV, 1), odd + pltpu.roll(odd, NV, 1)
        pair_ref[pair] = jnp.where(left_k, even, odd)
        for half in (0, 1):
            first = slice(half * TILE, half * TILE + ROWS)
            second = slice(half * TILE + ROWS, (half + 1) * TILE)
            rows = slice(half * ROWS, (half + 1) * ROWS)
            coef_ref[2 * pair, rows] = jnp.where(left_r, even[first], even[second])
            coef_ref[2 * pair + 1, rows] = jnp.where(left_r, odd[first], odd[second])


def leaf_coefs(basis, vectors, block):
    leaves = basis.shape[1] // PTS
    return pl.pallas_call(
        coef_kernel,
        out_shape=(
            jax.ShapeDtypeStruct((leaves, TILE, LANES), jnp.float32),
            jax.ShapeDtypeStruct((leaves // 2, K, LANES), jnp.float32),
        ),
        grid=(leaves // block,),
        in_specs=[
            pl.BlockSpec((K, block * PTS), lambda i: (0, i)),
            pl.BlockSpec((NV, block * PTS), lambda i: (0, i)),
        ],
        out_specs=(
            pl.BlockSpec((block, TILE, LANES), lambda i: (i, 0, 0)),
            pl.BlockSpec((block // 2, K, LANES), lambda i: (i, 0, 0)),
        ),
        compiler_params=pltpu.CompilerParams(vmem_limit_bytes=WHOLE_LIMIT),
        name="leaf_coef",
    )(basis, vectors)


def pick_slot(x, live, left_r):
    x = x * live.astype(jnp.float32)
    high = x.astype(jnp.bfloat16).astype(jnp.float32)
    low = pltpu.roll(x - high, NV, 1)
    return jnp.concatenate([jnp.where(left_r, high, low), jnp.where(left_r, low, high)], axis=0).astype(jnp.bfloat16)


def pick_kernel(plan, first, code_ref, *refs):
    sources, out_ref, held, sem = refs[:-3], refs[-3], refs[-2], refs[-1]
    step = pl.program_id(0)
    left_r = left_lanes(ROWS)

    @pl.when(step == 0)
    def _():
        for device, source, start, target, count in plan:
            pltpu.make_async_copy(
                sources[source].at[pl.ds(start, count)],
                held.at[device, pl.ds(target, count)],
                sem.at[device],
            ).start()

    pltpu.make_async_copy(held.at[step], held.at[step], sem.at[step]).wait()

    @pl.loop(0, CAP // 32)
    def _(part):
        for n in range(32):
            slot = part * 32 + n
            code = code_ref[first + step, slot]
            both = held[step, code >> 1]
            out_ref[slot, :TILE] = pick_slot(both[:ROWS], code & 1, left_r)
            out_ref[slot, TILE:] = pick_slot(both[ROWS:], code & 1, left_r)


def picked_slots(devices, codes, pieces, unit, leaves):
    first = ORDER.index(devices[0])
    arrays, plan = [], []
    for device, key in enumerate(devices):
        for quarter in range(QUARTERS):
            piece, at = next((p, p[1].index(key + (quarter,))) for p in pieces if key + (quarter,) in p[1])
            index = next((i for i, a in enumerate(arrays) if a is piece[0]), None)
            if index is None:
                index = len(arrays)
                arrays.append(piece[0])
            last = plan[-1] if plan else None
            if last and last[0] == device and last[1] == index and last[2] + last[4] == at * unit:
                plan[-1] = last[:4] + (last[4] + unit,)
            else:
                plan.append((device, index, at * unit, quarter * unit, unit))
    count = len(devices)
    return pl.pallas_call(
        functools.partial(pick_kernel, plan, first),
        out_shape=jax.ShapeDtypeStruct((count * CAP, K, LANES), jnp.bfloat16),
        grid=(count,),
        in_specs=[pl.BlockSpec(memory_space=pltpu.SMEM)] + [pl.BlockSpec(memory_space=pl.ANY)] * len(arrays),
        out_specs=pl.BlockSpec((CAP, K, LANES), lambda i: (i, 0, 0)),
        scratch_shapes=[
            pltpu.VMEM((count, leaves, TILE, LANES), jnp.float32),
            pltpu.SemaphoreType.DMA((count,)),
        ],
        compiler_params=pltpu.CompilerParams(vmem_limit_bytes=SMALL_LIMIT),
        cost_estimate=BRIEF,
        name="pick",
    )(codes, *arrays)


def arrival_plan(devices, pieces, unit):
    arrays, plan = [], []
    for rank, key in enumerate(devices):
        for quarter in range(QUARTERS):
            piece, at = next((p, p[1].index(key + (quarter,))) for p in pieces if key + (quarter,) in p[1])
            index = next((i for i, a in enumerate(arrays) if a is piece[0]), None)
            if index is None:
                index = len(arrays)
                arrays.append(piece[0])
            last = plan[-1] if plan else None
            if last and last[:2] == (rank, index) and last[2] + last[4] == at * unit:
                plan[-1] = last[:4] + (last[4] + unit,)
            else:
                plan.append((rank, index, at * unit, quarter * unit, unit))
    return arrays, plan


def field_kernel(slots, block, plan, ready, count, pos_ref, code_ref, *refs):
    pieces, sources = refs[:ready], refs[ready : ready + count]
    coupling_ref, down_ref, basis_ref, out_ref, tiles, held, totals, sem, held_sem = refs[ready + count :]
    step = pl.program_id(0)
    first = step * block
    left_k, left_r, left_v = left_lanes(K), left_lanes(ROWS), left_lanes(NV)

    @pl.when(step == 0)
    def _():
        for device, source, start, target, size in plan:
            pltpu.make_async_copy(
                sources[source].at[pl.ds(start, size)], held.at[device, pl.ds(target, size)], held_sem.at[device]
            ).start()
        copies, at = [], 0
        for piece in pieces:
            copies.append(pltpu.make_async_copy(piece, tiles.at[pl.ds(at, piece.shape[0])], sem.at[len(copies)]))
            at += piece.shape[0]
        for copy in copies:
            copy.start()
        early = at // CAP

        @pl.loop(0, held.shape[0])
        def _(device):
            pltpu.make_async_copy(held.at[device], held.at[device], held_sem.at[device]).wait()
            for slot in range(CAP):
                code = code_ref[early + device, slot]
                both = held[device, code >> 1]
                place = (early + device) * CAP + slot
                tiles[place, :TILE] = pick_slot(both[:ROWS], code & 1, left_r)
                tiles[place, TILE:] = pick_slot(both[ROWS:], code & 1, left_r)

        for copy in copies:
            copy.wait()

    def leaf_field(leaf):
        parts = [tiles[pos_ref[first + leaf, slot]] for slot in range(slots)]
        both = jnp.dot(
            jnp.concatenate(split(coupling_ref[leaf]), axis=0),
            jnp.concatenate(parts, axis=0),
            preferred_element_type=jnp.float32,
        )
        summed = both[:K] + both[K:]
        return summed + pltpu.roll(summed, NV, 1)

    def pair_total(pair):
        return jnp.where(left_k, leaf_field(2 * pair), leaf_field(2 * pair + 1)) + down_ref[pair]

    def diagonal(x):
        rows = []
        for g in range(4):
            row = [x[:, n * LANES : (n + 1) * LANES] if n == g else jnp.zeros((K, LANES), x.dtype) for n in range(4)]
            rows.append(jnp.concatenate(row, axis=1))
        return jnp.concatenate(rows, axis=0)

    def product(quad, total):
        high, low = split(total.T)
        at = pl.multiple_of(quad * 4 * LANES, 4 * LANES)
        basis_high, basis_low = split(basis_ref[:, pl.ds(at, 4 * LANES)])
        spread = diagonal(basis_high)
        both = jnp.dot(
            jnp.concatenate([high, low], axis=1),
            jnp.concatenate([spread, spread], axis=0),
            preferred_element_type=jnp.float32,
        )
        both += jnp.dot(high, diagonal(basis_low), preferred_element_type=jnp.float32)
        for n in range(4):
            square = both[:, n * LANES : (n + 1) * LANES]
            out_ref[:, pl.ds(pl.multiple_of(at + n * LANES, LANES), LANES)] = jnp.where(
                left_v, square[:NV], square[NV:]
            )

    quads = block // 8
    totals_first = step * quads

    @pl.when(step == 0)
    def _():
        totals[...] = jnp.zeros_like(totals)

    @pl.loop(0, quads // 4)
    def _(turn):
        for n in range(4):
            quad = totals_first + 4 * turn + n
            before = totals[1 - n % 2]
            for pair in range(4):
                totals[n % 2, pair * K : (pair + 1) * K] = pair_total(16 * turn + 4 * n + pair)
            product(jnp.maximum(quad - 1, 0), before)

    @pl.when(step == pl.num_programs(0) - 1)
    def _():
        product(totals_first + quads - 1, totals[1])


def products(pos, codes, tiles, late, pieces, coupling, down, basis, block):
    leaves, _, width = coupling.shape
    slots = width // K
    arrays, plan = arrival_plan(late, pieces, leaves // QUARTERS)
    smem, hbm = pl.BlockSpec(memory_space=pltpu.SMEM), pl.BlockSpec(memory_space=pl.ANY)
    return pl.pallas_call(
        functools.partial(field_kernel, slots, block, plan, len(tiles), len(arrays)),
        out_shape=jax.ShapeDtypeStruct((NV, leaves * PTS), jnp.float32),
        grid=(leaves // block,),
        in_specs=[smem, smem]
        + [hbm] * (len(tiles) + len(arrays))
        + [
            pl.BlockSpec((block, K, width), lambda i: (i, 0, 0)),
            pl.BlockSpec((block // 2, K, LANES), lambda i: (i, 0, 0)),
            pl.BlockSpec((K, leaves * PTS), lambda i: (0, 0)),
        ],
        out_specs=pl.BlockSpec((NV, leaves * PTS), lambda i: (0, 0)),
        scratch_shapes=[
            pltpu.VMEM((leaves * slots, K, LANES), jnp.bfloat16),
            pltpu.VMEM((len(late), leaves, TILE, LANES), jnp.float32),
            pltpu.VMEM((2, 4 * K, LANES), jnp.float32),
            pltpu.SemaphoreType.DMA((len(tiles),)),
            pltpu.SemaphoreType.DMA((len(late),)),
        ],
        compiler_params=pltpu.CompilerParams(vmem_limit_bytes=FINAL_LIMIT),
        cost_estimate=BRIEF,
        name="leaf_field_product",
    )(pos, codes, *tiles, *arrays, coupling, down, basis)


def subtree_index(dy, dz, flip, z, y, core):
    return (z + dz) % SIDE * (2 * SIDE) + (y + dy) % SIDE * 2 + (core + flip) % 2


def moved(piece, axis, by, send):
    array, segs = piece
    perm, out = [], []
    for z in range(SIDE):
        for y in range(SIDE):
            for core in range(2):
                step = {"y": (by, 0, 0), "z": (0, by, 0), "core": (0, 0, 1)}[axis]
                perm.append((subtree_index(0, 0, 0, z, y, core), subtree_index(*step, z, y, core)))
    for dy, dz, flip, quarter in segs:
        if axis == "y":
            out.append(((dy - by) % SIDE, dz, flip, quarter))
        elif axis == "z":
            out.append((dy, (dz - by) % SIDE, flip, quarter))
        else:
            out.append((dy, dz, 1 - flip, quarter))
    return send(array, "subtree", perm), out


class Turns:
    def __init__(self):
        self.last = None

    def __call__(self, array, axis, perm, after=()):
        if self.last is not None:
            array, _ = lax.optimization_barrier((array, (self.last, after)))
        self.last = lax.ppermute(array, axis, perm)
        return self.last


def pack_kernel(plan, count, *refs):
    sources, targets, (held, read_sem, write_sem) = refs[:count], refs[count:-3], refs[-3:]
    reads, writes, base = [], [], 0
    for number, (source, start, target, at, size) in enumerate(plan):
        place = held.at[pl.ds(base, size)]
        reads.append(pltpu.make_async_copy(sources[source].at[pl.ds(start, size)], place, read_sem.at[number]))
        writes.append(pltpu.make_async_copy(place, targets[target].at[pl.ds(at, size)], write_sem.at[number]))
        base += size
    for read in reads:
        read.start()
    for read, write in zip(reads, writes, strict=True):
        read.wait()
        write.start()
    for write in writes:
        write.wait()


def packed(pieces, wanted, unit, cost=BRIEF):
    arrays, plan = [], []
    for target, keys in enumerate(wanted):
        for at, key in enumerate(keys):
            piece = next(p for p in pieces if key in p[1])
            source = next((i for i, a in enumerate(arrays) if a is piece[0]), None)
            if source is None:
                source = len(arrays)
                arrays.append(piece[0])
            start = piece[1].index(key) * unit
            last = plan[-1] if plan else None
            if last and last[0] == source and last[2] == target and last[1] + last[4] == start:
                plan[-1] = last[:4] + (last[4] + unit,)
            else:
                plan.append((source, start, target, at * unit, unit))
    shapes = tuple(
        jax.ShapeDtypeStruct((len(keys) * unit,) + arrays[0].shape[1:], arrays[0].dtype) for keys in wanted
    )
    any_space = pl.BlockSpec(memory_space=pl.ANY)
    out = pl.pallas_call(
        functools.partial(pack_kernel, plan, len(arrays)),
        out_shape=shapes,
        in_specs=[any_space] * len(arrays),
        out_specs=(any_space,) * len(shapes),
        scratch_shapes=[
            pltpu.VMEM((sum(shape.shape[0] for shape in shapes),) + arrays[0].shape[1:], arrays[0].dtype),
            pltpu.SemaphoreType.DMA((len(plan),)),
            pltpu.SemaphoreType.DMA((len(plan),)),
        ],
        compiler_params=pltpu.CompilerParams(vmem_limit_bytes=SMALL_LIMIT),
        cost_estimate=cost,
        name="pack",
    )(*arrays)
    return [(array, list(keys)) for array, keys in zip(out, wanted, strict=True)]


def segs(dy, dz, quarters):
    return [(dy % SIDE, dz % SIDE, 0, q) for q in quarters]


FIRST, SECOND = (0, 1), (2, 3)
SENDS = [
    [("y", 1, segs(0, 0, range(4))), ("y", -1, segs(0, 0, range(4))), ("z", 1, segs(0, 0, range(4))), ("z", -1, segs(0, 0, range(4)))],
    [
        ("z", 1, segs(1, 0, FIRST) + segs(-1, 0, FIRST) + segs(0, -1, FIRST)),
        ("z", -1, segs(1, 0, FIRST) + segs(-1, 0, FIRST) + segs(0, 1, SECOND)),
        ("y", 1, segs(0, 1, SECOND) + segs(0, -1, SECOND) + segs(-1, 0, FIRST)),
        ("y", -1, segs(0, 1, SECOND) + segs(0, -1, SECOND) + segs(1, 0, SECOND)),
    ],
    [
        ("z", 1, segs(2, 0, FIRST) + segs(1, -1, (0,)) + segs(-1, -1, (0,))),
        ("z", -1, segs(2, 0, FIRST) + segs(1, 1, (1,)) + segs(-1, 1, (1,))),
        ("y", 1, segs(0, 2, SECOND) + segs(-1, 1, (2,)) + segs(-1, -1, (2,))),
        ("y", -1, segs(0, 2, SECOND) + segs(1, 1, (3,)) + segs(1, -1, (3,))),
    ],
    [("z", 1, segs(2, -1, (0,))), ("z", -1, segs(2, 1, (1,))), ("y", 1, segs(-1, 2, (2,))), ("y", -1, segs(1, 2, (3,)))],
]


def ring(own, leaves, turns, beside):
    unit = leaves // QUARTERS
    mine = (own, segs(0, 0, range(QUARTERS)))
    have, others, fresh, done = [mine], [], [mine], []
    payloads = [mine] * len(SENDS[0])
    for number, sends in enumerate(SENDS):
        new = [moved(p, axis, by, lax.ppermute) for p, (axis, by, _) in zip(payloads, sends, strict=True)]
        joined = fresh[0]
        if number > 0:
            joined = packed(fresh, [[key for p in fresh for key in p[1]]], unit)[0]
        swapped = moved(joined, "core", 1, turns)
        done = beside[number](have, others, done)
        if number + 1 < len(SENDS):
            following = packed(have + new, [keys for _, _, keys in SENDS[number + 1]], unit, LONG)
        else:
            following = packed(new, [[key for p in new for key in p[1]]], unit)
        arrays, ahead, other, done = lax.optimization_barrier(
            ([p[0] for p in new], [p[0] for p in following], swapped[0], done)
        )
        fresh = [(array, p[1]) for array, p in zip(arrays, new, strict=True)]
        payloads = [(array, p[1]) for array, p in zip(ahead, following, strict=True)]
        have, others = have + fresh, others + [(other, swapped[1])]
    return have + others + [moved(payloads[0], "core", 1, lax.ppermute)], done


def order_kernel(own_ref, list_ref, mask_ref, pos_ref, code_ref):
    leaves, slots = list_ref.shape
    devices = len(ORDER)
    names = list_ref[...]
    owner = lax.rem(names // leaves, devices)
    code = (lax.rem(names, leaves) * 2 + mask_ref[...]).astype(jnp.float32)
    row = lax.broadcasted_iota(jnp.int32, (leaves, LANES), 0)
    lane = lax.broadcasted_iota(jnp.int32, (leaves, LANES), 1)
    below = (row > lane).astype(jnp.bfloat16)
    own = jnp.broadcast_to(own_ref[...], (leaves, LANES))
    used = jnp.zeros((1, LANES), jnp.float32)
    sorted_codes = jnp.zeros((LANES, LANES), jnp.float32)
    places = jnp.zeros((leaves, LANES), jnp.float32)
    for slot in range(slots):
        named = (owner[:, slot : slot + 1] == own).astype(jnp.float32)
        before = jnp.dot(below, named.astype(jnp.bfloat16), preferred_element_type=jnp.float32) + used
        used = used + jnp.sum(named, axis=0, keepdims=True)
        index = jnp.sum(named * before, axis=1, keepdims=True)
        rank = jnp.sum(named * lane.astype(jnp.float32), axis=1, keepdims=True)
        places = jnp.where(lane == slot, rank * CAP + index, places)
        spread = (lane.astype(jnp.float32) == index).astype(jnp.bfloat16)
        sorted_codes = sorted_codes + lax.dot_general(
            (named * code[:, slot : slot + 1]).astype(jnp.bfloat16),
            spread,
            (((0,), (0,)), ((), ())),
            preferred_element_type=jnp.float32,
        )
    pos_ref[...] = places[:, :slots].astype(jnp.int32)
    code_ref[...] = sorted_codes[:devices].astype(jnp.int32)


def slot_order(leaf_list, leaf_mask, own):
    return pl.pallas_call(
        order_kernel,
        out_shape=(
            jax.ShapeDtypeStruct(leaf_list.shape, jnp.int32),
            jax.ShapeDtypeStruct((len(ORDER), LANES), jnp.int32),
        ),
        compiler_params=pltpu.CompilerParams(vmem_limit_bytes=SMALL_LIMIT),
        cost_estimate=BRIEF,
        name="slot_order",
    )(own, leaf_list, leaf_mask)


def parent_coef_kernel(pair_ref, transfer_ref, out_ref):
    left_r = left_lanes(ROWS)
    for parent in range(out_ref.shape[0]):
        blocks = []
        for leaf in range(CHILD):
            pair = parent * CHILD // 2 + leaf // 2
            x = [pair_ref[pair, pl.ds(a4, ROWS, stride=4), :] for a4 in range(4)]
            if leaf % 2 == 0:
                tiles = [jnp.where(left_r, x[n], pltpu.roll(x[n + 1], NV, 1)) for n in (0, 2)]
            else:
                tiles = [jnp.where(left_r, pltpu.roll(x[n], NV, 1), x[n + 1]) for n in (0, 2)]
            blocks.append(jnp.concatenate(tiles, axis=1))
        coef_high, coef_low = split(jnp.concatenate(blocks, axis=0))
        rows = CHILD * ROWS
        high, low = split(transfer_ref[parent * rows : (parent + 1) * rows])
        full = lax.dot_general(
            jnp.concatenate([high, low, high], axis=0),
            jnp.concatenate([coef_high, coef_high, coef_low], axis=0),
            (((0,), (0,)), ((), ())),
            preferred_element_type=jnp.float32,
        )
        even = full[:K, :LANES] + full[2 * K : 3 * K, LANES:]
        odd = full[K : 2 * K, :LANES] + full[3 * K :, LANES:]
        total = even + pltpu.roll(odd, NV, 1)
        for half in (0, 1):
            first = total[half * TILE : half * TILE + ROWS]
            second = total[half * TILE + ROWS : (half + 1) * TILE]
            out_ref[parent, half * ROWS : (half + 1) * ROWS] = jnp.where(left_r, first, pltpu.roll(second, NV, 1))


def parent_coefs(coef_pairs, rows):
    parents = coef_pairs.shape[0] * 2 // CHILD
    return pl.pallas_call(
        parent_coef_kernel,
        out_shape=jax.ShapeDtypeStruct((parents, TILE, LANES), jnp.float32),
        compiler_params=pltpu.CompilerParams(vmem_limit_bytes=SMALL_LIMIT),
        cost_estimate=BRIEF,
        name="parent_coef",
    )(coef_pairs, rows)


def parent_field_kernel(group, list_ref, mask_ref, branch_ref, *refs):
    coef_refs, (coupling_ref, transfer_ref, down_ref, coef_ref) = refs[:BRANCHES], refs[BRANCHES:]
    parents = coef_ref.shape[0] // BRANCHES
    slots = list_ref.shape[1]
    parent = pl.program_id(0)
    left_k, left_r = left_lanes(K), left_lanes(ROWS)

    @pl.when(parent == 0)
    def _():
        for number, ref in enumerate(coef_refs):
            coef_ref[number * parents : (number + 1) * parents] = ref[...]

    parts = []
    for slot in range(slots):
        name = list_ref[parent, slot]
        at = lax.rem(name // group - branch_ref[0] + BRANCHES, BRANCHES) * parents + lax.rem(name, parents)
        both = coef_ref[at]
        live = mask_ref[parent, slot]
        parts += [pick_slot(both[:ROWS], live, left_r), pick_slot(both[ROWS:], live, left_r)]
    both = jnp.dot(
        jnp.concatenate(split(coupling_ref[0]), axis=0),
        jnp.concatenate(parts, axis=0),
        preferred_element_type=jnp.float32,
    )
    summed = both[:K] + both[K:]
    field = summed + pltpu.roll(summed, NV, 1)
    zero = jnp.zeros_like(field)
    left, right = jnp.where(left_k, field, zero), jnp.where(left_k, zero, field)
    spread = jnp.concatenate(
        [
            jnp.concatenate([left, right, zero, zero], axis=0),
            jnp.concatenate([zero, zero, left, right], axis=0),
        ],
        axis=1,
    )
    spread_high, spread_low = split(spread)
    high, low = split(transfer_ref[...])
    full = jnp.dot(
        jnp.concatenate([high, low, high], axis=1),
        jnp.concatenate([spread_high, spread_high, spread_low], axis=0),
        preferred_element_type=jnp.float32,
    )
    for pair in range(CHILD // 2):
        for a4 in range(4):
            lanes = slice(a4 // 2 * LANES, (a4 // 2 + 1) * LANES)
            even = full[2 * pair * ROWS : (2 * pair + 1) * ROWS, lanes]
            odd = full[(2 * pair + 1) * ROWS : (2 * pair + 2) * ROWS, lanes]
            if a4 % 2 == 0:
                odd = pltpu.roll(odd, NV, 1)
            else:
                even = pltpu.roll(even, NV, 1)
            down_ref[pair, pl.ds(a4, ROWS, stride=4), :] = jnp.where(left_r, even, odd)


def downward_pairs(parent_list, parent_mask, branch, group, coef_all, coupling, rows):
    parents, _, width = coupling.shape
    smem = pl.BlockSpec(memory_space=pltpu.SMEM)
    return pl.pallas_call(
        functools.partial(parent_field_kernel, group),
        out_shape=jax.ShapeDtypeStruct((parents * CHILD // 2, K, LANES), jnp.float32),
        grid=(parents,),
        in_specs=[
            smem,
            smem,
            smem,
        ]
        + [pl.BlockSpec(memory_space=pltpu.VMEM)] * BRANCHES
        + [
            pl.BlockSpec((1, K, width), lambda i: (i, 0, 0)),
            pl.BlockSpec((CHILD * ROWS, LANES), lambda i: (i, 0)),
        ],
        out_specs=pl.BlockSpec((CHILD // 2, K, LANES), lambda i: (i, 0, 0)),
        scratch_shapes=[pltpu.VMEM((BRANCHES * parents, TILE, LANES), jnp.float32)],
        compiler_params=pltpu.CompilerParams(vmem_limit_bytes=SMALL_LIMIT),
        cost_estimate=BRIEF,
        name="parent_field",
    )(parent_list, parent_mask, branch, *coef_all, coupling, rows)


def per_device(
    vectors,
    basis,
    transfer,
    leaf_coupling,
    leaf_list,
    leaf_mask,
    parent_coupling,
    parent_list,
    parent_mask,
):
    leaf_count = leaf_list.shape[0]
    parent_count = parent_list.shape[0]
    subtrees = lax.axis_size("subtree")
    branches = lax.axis_size("branch")
    me = lax.axis_index("subtree")
    here = (me // (2 * SIDE), me // 2 % SIDE, me % 2)

    own = jnp.stack([subtree_index(dy, dz, flip, *here) for dy, dz, flip in ORDER]).astype(jnp.int32)
    own = jnp.pad(own, (0, LANES - len(ORDER)), constant_values=-1)[None, :]
    branch = lax.axis_index("branch").astype(jnp.int32)[None]
    rows = transfer.reshape(parent_count * CHILD * ROWS, LANES)
    coef, coef_pairs = leaf_coefs(basis, vectors, 64)
    turns = Turns()

    def pick(number, flips, codes, pieces):
        devices = [key + (flip,) for flip in flips for key in STAGES[number]]
        return picked_slots(devices, codes, pieces, leaf_count // QUARTERS, leaf_count)

    def beside_first(have, others, done):
        parent_coef = parent_coefs(coef_pairs, rows)
        coef_all = [parent_coef]
        order = ()
        for by in range(1, branches):
            perm = [(i, (i - by) % branches) for i in range(branches)]
            coef_all.append(turns(parent_coef, "branch", perm, order))
            if by == 1:
                order = slot_order(leaf_list, leaf_mask, own)
        return order, coef_all

    def beside_second(have, others, done):
        order, coef_all = done
        down = downward_pairs(
            parent_list, parent_mask, branch, parent_count * subtrees, coef_all, parent_coupling, rows
        )
        return order, down, [pick(0, (0,), order[1], have)]

    def beside_third(have, others, done):
        order, down, tiles = done
        far = pick(0, (1,), order[1], others)
        return order, down, tiles + [far, pick(1, (0,), order[1], have)]

    def beside_fourth(have, others, done):
        order, down, tiles = done
        return order, down, tiles + [pick(1, (1,), order[1], others)]

    pieces, ((pos, codes), down, tiles) = ring(
        coef, leaf_count, turns, [beside_first, beside_second, beside_third, beside_fourth]
    )
    tiles = tiles + [pick(2, (0,), codes, pieces)]
    late = ORDER[2 * (len(STAGES[0]) + len(STAGES[1])) + len(STAGES[2]) :]
    return products(pos, codes, tiles, late, pieces, leaf_coupling, down, basis, 32)


def solution(mesh):
    return jax.shard_map(
        per_device,
        mesh=mesh,
        in_specs=(
            P(None, ("branch", "subtree")),
            P(None, ("branch", "subtree")),
            P(("branch", "subtree"), None),
            P(("branch", "subtree"), None, None),
            P(("branch", "subtree"), None),
            P(("branch", "subtree"), None),
            P(("branch", "subtree"), None, None),
            P(("branch", "subtree"), None),
            P(("branch", "subtree"), None),
        ),
        out_specs=P(None, ("branch", "subtree")),
        check_vma=False,
    )
```
